256 devices in a mesh: stn: 128 (over z, x_lo, y, core), tm: 2 (over x_hi).
Axes of the slice: x: 4 (x_hi: 2, x_lo: 2; x = x_hi * 2 + x_lo), y: 4, z: 8, core: 2. Of those that a mesh axis runs over, the one named last changes fastest.
Arguments:
- samples: bfloat16 [512, 2, 2, 131072], P('stn', None, None, 'tm'), may hold values from -6 to 6
- taps: float32 [12, 4096], replicated, may hold values from -1.8 to 1.8
- codes: int32 [64, 512], replicated, may hold values from 0 to 4095
- flags: int32 [512], replicated, may hold values 0 or 1
Outputs:
- beams: bfloat16 [4096, 2, 32, 128], P('stn', None, 'tm')
The draws below stay inside these ranges and needn't reach their ends.
All inputs are finite; a program needn't handle non-finite values.
Results may differ from the reference program's by a relative error of at most 0.0077.
Values may be sent and summed in bfloat16 or wider, within the bound.
No kernel may reach another device: no remote copies, remote signals or barrier semaphores. Data moves between devices by JAX's collectives and lax.ppermute only.
A program may use at most 64 MiB of HBM per device.

```python
import jax
import jax.numpy as jnp
from jax import lax

RADIX_A = 32
RADIX_B = 128
TAPS = 12
BEAMS = 64
NFFT = 4096
STATIONS = 512
SPECTRA = 32
CHAN_DEV = 32
N_STN = 128


def plant(drawn, stream_key, low, top_value):
    longest = drawn.shape.index(max(drawn.shape))
    spots = []
    for shift in (0, 1):
        where = [jax.random.randint(jax.random.fold_in(stream_key, axis), (), 0, length) for axis, length in enumerate(drawn.shape)]
        where[longest] = (where[longest] + shift) % drawn.shape[longest]
        spots.append(tuple(where))
    return drawn.at[spots[0]].set(low).at[spots[1]].set(top_value)


def levels(key, extent, cuts, least, high):
    def one(dim, parts):
        draws = jax.random.uniform(jax.random.fold_in(jax.random.fold_in(key, 6), dim), (parts,), jnp.float32, least / len(cuts), high / len(cuts))
        return jnp.repeat(jnp.exp(draws), extent[dim] // parts).reshape((-1,) + (1,) * (len(extent) - dim - 1))

    loudness = one(*cuts[0])
    for cut in cuts[1:]:
        loudness = loudness * one(*cut)
    return loudness


def scatter_about(rng, dims, width, most, pieces=(), kind=jnp.bfloat16):
    gain = levels(rng, dims, pieces, -0.22, 0.18) if pieces else 1.0
    values = jax.random.normal(rng, dims, jnp.float32) * width * gain
    return jnp.minimum(jnp.maximum(values, -most), most).astype(kind)


def setup_inputs(seed: int = 0) -> dict:
    splits = jax.random.split(jax.random.key(seed), 5)
    samples = scatter_about(splits[0], (STATIONS, 2, 2, SPECTRA * NFFT), 1.0, 6.0, ((0, 128), (3, 2)))
    taps = scatter_about(splits[1], (TAPS, NFFT), 0.3, 1.8, (), jnp.float32)
    codes = plant(jax.random.randint(splits[2], (BEAMS, STATIONS), 0, NFFT), jax.random.fold_in(splits[2], 1), 0, NFFT - 1).astype(jnp.int32)
    flags = plant((jax.random.randint(splits[3], (STATIONS,), 0, 4) < 3).astype(jnp.int32), jax.random.fold_in(splits[3], 1), 0, 1)
    return dict(samples=samples, taps=taps, codes=codes, flags=flags)


def dft_table(radix):
    indices = jnp.arange(radix, dtype=jnp.int32)
    angles = (indices[:, None] * indices[None, :] % radix).astype(jnp.float32) * (2.0 * jnp.pi / radix)
    cosine = jnp.cos(angles).astype(jnp.bfloat16)
    sine = jnp.sin(angles).astype(jnp.bfloat16)
    return jnp.stack([jnp.stack([cosine, -sine], axis=1), jnp.stack([sine, cosine], axis=1)], axis=0)

def twiddle_table(outer, inner):
    length = outer * inner
    rows = jnp.arange(outer, dtype=jnp.int32)
    cols = jnp.arange(inner, dtype=jnp.int32)
    angles = (rows[:, None] * cols[None, :] % length).astype(jnp.float32) * (2.0 * jnp.pi / length)
    return (jnp.cos(angles), jnp.sin(angles))

def beam_weights(codes, flags, channels, length, stations_all):
    phase = channels[:, :, None, None] * jnp.transpose(codes)[None, None, :, :] % length
    angles = phase.astype(jnp.float32) * (2.0 * jnp.pi / length)
    scale = flags.astype(jnp.float32) / jnp.sqrt(jnp.float32(stations_all))
    real_part = (jnp.cos(angles) * scale[None, None, :, None]).astype(jnp.bfloat16)
    imag_part = (-jnp.sin(angles) * scale[None, None, :, None]).astype(jnp.bfloat16)
    first_row = jnp.stack([real_part, imag_part], axis=3)
    second_row = jnp.stack([-imag_part, real_part], axis=3)
    return jnp.stack([first_row, second_row], axis=2)

def reference(samples, taps, codes, flags):
    table_outer = dft_table(RADIX_A).astype(jnp.float32)
    table_inner = dft_table(RADIX_B).reshape(2 * RADIX_B, 2 * RADIX_B).astype(jnp.float32)
    tw_cos, tw_sin = twiddle_table(RADIX_A, RADIX_B)
    tw_cos = tw_cos[:, None, None, :]
    tw_sin = tw_sin[:, None, None, :]
    norm = jnp.sqrt(jnp.float32(NFFT))
    taps_grid = taps.reshape(TAPS, RADIX_A, RADIX_B)

    def one_station(station):
        frames = station.reshape(2, 2, SPECTRA, RADIX_A, RADIX_B).astype(jnp.float32)
        padded = jnp.concatenate([jnp.zeros((2, 2, TAPS - 1, RADIX_A, RADIX_B), jnp.float32), frames], axis=2)
        filtered = jnp.zeros((2, 2, SPECTRA, RADIX_A, RADIX_B), jnp.float32)
        for tap in range(TAPS):
            filtered = filtered + taps_grid[tap][None, None, None] * padded[:, :, tap:tap + SPECTRA]
        filtered = filtered.astype(jnp.bfloat16).astype(jnp.float32)
        first = jnp.einsum('iaoc,pifab->ocpfb', table_outer, filtered)
        real_in = first[0]
        imag_in = first[1]
        real_out = (real_in * tw_cos + imag_in * tw_sin) / norm
        imag_out = (imag_in * tw_cos - real_in * tw_sin) / norm
        middle = jnp.concatenate([real_out, imag_out], axis=-1).astype(jnp.bfloat16).astype(jnp.float32)
        second = jnp.einsum('cpfk,kn->cpfn', middle, table_inner)
        return second.reshape(RADIX_A, 2, SPECTRA, 2, RADIX_B).astype(jnp.bfloat16)
    spectra = lax.map(one_station, samples)
    digits = RADIX_B // N_STN

    def one_block(block):
        upper = block * digits + jnp.arange(digits, dtype=jnp.int32)
        channels = jnp.arange(RADIX_A, dtype=jnp.int32)[None, :] + RADIX_A * upper[:, None]
        weights = beam_weights(codes, flags, channels, NFFT, STATIONS).astype(jnp.float32)
        part = lax.dynamic_slice_in_dim(spectra, block * digits, digits, axis=5).astype(jnp.float32)
        result = jnp.einsum('scpfoe,ecosrb->ecpfrb', part, weights)
        return result.reshape(CHAN_DEV, 2, SPECTRA, 2 * BEAMS)
    blocks = lax.map(one_block, jnp.arange(N_STN, dtype=jnp.int32))
    return blocks.reshape(NFFT, 2, SPECTRA, 2 * BEAMS).astype(jnp.bfloat16)
```

```python
import functools

import jax
import jax.numpy as jnp
import ml_dtypes
import numpy as np
from jax import lax
from jax.experimental import pallas as pl
from jax.experimental.pallas import tpu as pltpu
from jax.sharding import PartitionSpec as P

RADIX_A = 32
RADIX_B = 128
TAPS = 12
LENGTH = RADIX_A * RADIX_B
ROWS = 2 * RADIX_A
QUAD = 4
BF16 = jnp.bfloat16
F32 = jnp.float32
VMEM_LIMIT = 48 << 20


def dft_table(radix):
    indices = np.arange(radix)
    angles = (indices[:, None] * indices[None, :] % radix) * (2.0 * np.pi / radix)
    cosine = np.cos(angles).astype(ml_dtypes.bfloat16)
    sine = np.sin(angles).astype(ml_dtypes.bfloat16)
    return np.stack(
        [np.stack([cosine, -sine], axis=1), np.stack([sine, cosine], axis=1)], axis=0
    )


def outer_table():
    table = dft_table(RADIX_A)
    grid = np.zeros((2, RADIX_A, QUAD, QUAD, RADIX_A, 2), ml_dtypes.bfloat16)
    for i in range(QUAD):
        grid[:, :, i, i] = table.transpose(2, 3, 1, 0)
    return grid.reshape(2 * RADIX_A * QUAD, QUAD * ROWS)


def inner_table():
    return dft_table(RADIX_B).reshape(2 * RADIX_B, 2 * RADIX_B).T.copy()


def twiddles():
    c1 = np.repeat(np.arange(RADIX_A), QUAD)
    angles = (c1[:, None] * np.arange(RADIX_B)[None, :] % LENGTH) * (2.0 * np.pi / LENGTH)
    scale = 1.0 / np.sqrt(np.float64(LENGTH))
    return np.stack([np.cos(angles) * scale, np.sin(angles) * scale]).astype(np.float32)


def channelise_body(first, count, quads, *refs):
    if first < TAPS - 1:
        x_ref, halo_ref, taps_ref, outer_ref, tw_ref, inner_ref, out_ref, taps2, filt, mid, turn = refs
    else:
        x_ref, taps_ref, outer_ref, tw_ref, inner_ref, out_ref, taps2, filt, mid, turn = refs
        halo_ref = None
    station = pl.program_id(0)
    groups = quads
    block = 8 * groups

    @pl.when(station == 0)
    def _():
        for a in range(RADIX_A):
            for k in range(TAPS):
                row = taps_ref[k : k + 1, a * RADIX_B : (a + 1) * RADIX_B]
                taps2[k, 2 * a : 2 * a + 2, :] = jnp.broadcast_to(row, (2, RADIX_B))

    def fir(step, carry):
        pol = step // (ROWS // 16)
        row = pl.multiple_of(step % (ROWS // 16) * 16, 16)
        frames = []
        for f in range(first - TAPS + 1, first + count):
            if f < 0:
                at = pl.multiple_of((f + TAPS - 1) * ROWS + row, 16)
                piece = halo_ref[0, pol, pl.ds(at, 16), :]
            else:
                at = pl.multiple_of(f * ROWS + row, 16)
                piece = x_ref[0, pol, pl.ds(at, 16), :]
            frames.append(piece.astype(F32))
        taps = [taps2[k, pl.ds(row, 16), :] for k in range(TAPS)]
        halves = []
        for half in range(2):
            rows = slice(8 * half, 8 * half + 8)
            outs = []
            for t in range(count):
                total = taps[0][rows] * frames[t][rows]
                for k in range(1, TAPS):
                    total = total + taps[k][rows] * frames[t + k][rows]
                outs.append(total)
            halves.append(outs)
        for t in range(count):
            both = jnp.concatenate([halves[0][t], halves[1][t]], axis=0).astype(BF16)
            at = pl.multiple_of((pol * count + t) * ROWS + row, 16)
            filt[pl.ds(at, 16), :] = both
        return carry

    lax.fori_loop(0, 2 * (ROWS // 16), fir, 0)

    cosine = tw_ref[0]
    sine = tw_ref[1]
    half = RADIX_A * QUAD
    for q in range(quads):
        data = filt[q * QUAD * ROWS : (q + 1) * QUAD * ROWS, :]
        got = jnp.dot(outer_ref[...], data, preferred_element_type=F32)
        real = got[:half]
        imag = got[half:]
        real_out = (real * cosine + imag * sine).astype(BF16)
        imag_out = (imag * cosine - real * sine).astype(BF16)
        for g in range(half // 16):
            at = (g * quads + q) * 16
            mid[at : at + 16, :RADIX_B] = real_out[16 * g : 16 * g + 16]
            mid[at : at + 16, RADIX_B:] = imag_out[16 * g : 16 * g + 16]

    for pair in range(groups // 2):
        data = mid[pair * 256 : pair * 256 + 256, :]
        got = lax.dot_general(
            inner_ref[...], data, (((1,), (1,)), ((), ())), preferred_element_type=F32
        )
        for side in range(2):
            group = 2 * pair + side
            for part in range(2):
                for c in range(0, RADIX_B, 8):
                    start = c * block + group * 8 + part + 2 * station
                    turn[pl.ds(start, 8, stride=block), :] = got[
                        part * RADIX_B + c : part * RADIX_B + c + 8,
                        side * 128 : side * 128 + 128,
                    ]

    @pl.when(station == pl.num_programs(0) - 1)
    def _():
        def turn_out(step, carry):
            at = pl.multiple_of(step * 256, 256)
            out_ref[pl.ds(at, 256), :] = turn[pl.ds(at, 256), :].astype(BF16)
            return carry

        lax.fori_loop(0, RADIX_B * block // 256, turn_out, 0)


def channelise(x, halo, taps, tables, first, count):
    stations = x.shape[0]
    quads = 2 * count // QUAD
    rows = RADIX_B * 8 * quads

    def whole(array):
        return pl.BlockSpec(array.shape, lambda s: (0,) * array.ndim)

    operands = [x]
    in_specs = [pl.BlockSpec((1,) + x.shape[1:], lambda s: (s, 0, 0, 0))]
    if halo is not None:
        operands.append(halo)
        in_specs.append(pl.BlockSpec((1,) + halo.shape[1:], lambda s: (s, 0, 0, 0)))
    for array in (taps,) + tables:
        operands.append(array)
        in_specs.append(whole(array))
    return pl.pallas_call(
        functools.partial(channelise_body, first, count, quads),
        grid=(stations,),
        out_shape=jax.ShapeDtypeStruct((rows, 128), BF16),
        in_specs=in_specs,
        out_specs=pl.BlockSpec((rows, 128), lambda s: (0, 0)),
        scratch_shapes=[
            pltpu.VMEM((TAPS, ROWS, RADIX_B), F32),
            pltpu.VMEM((2 * count * ROWS, RADIX_B), BF16),
            pltpu.VMEM((128 * quads, 2 * RADIX_B), BF16),
            pltpu.VMEM((rows, 128), F32),
        ],
        compiler_params=pltpu.CompilerParams(vmem_limit_bytes=VMEM_LIMIT),
        cost_estimate=pl.CostEstimate(
            flops=2 * 2 * stations * count * LENGTH * (4 * 64 + 256 + 24),
            bytes_accessed=2 * x.size + 2 * rows * 128,
            transcendentals=0,
        ),
    )(*operands)


def weights_body(upper_ref, codes_ref, scale_ref, out_ref):
    upper = upper_ref[0]
    unit = 2.0 * np.pi / LENGTH

    def step(at, carry):
        row = pl.multiple_of(at // 8 * 16, 16)
        col = pl.multiple_of(at % 8 * 128, 128)
        codes = codes_ref[pl.ds(row, 16), pl.ds(col, 128)]
        scale = scale_ref[:, pl.ds(col, 128)]
        start = ((codes * (upper * RADIX_A)) & (LENGTH - 1)).astype(F32) * unit
        by = codes.astype(F32) * unit
        odd = (lax.broadcasted_iota(jnp.int32, (16, 128), 1) & 1) == 1
        cosine = jnp.cos(start) * scale
        sine = jnp.sin(start) * scale
        upper_row = jnp.where(odd, sine, cosine)
        lower_row = jnp.where(odd, cosine, -sine)
        by_cos = jnp.cos(by)
        by_sin = jnp.sin(by)
        for c1 in range(RADIX_A):
            out_ref[c1, pl.ds(row, 16), pl.ds(col, 128)] = upper_row.astype(BF16)
            out_ref[c1, pl.ds(row + 64, 16), pl.ds(col, 128)] = lower_row.astype(BF16)
            if c1 + 1 < RADIX_A:
                upper_row, lower_row = (
                    upper_row * by_cos + lower_row * by_sin,
                    lower_row * by_cos - upper_row * by_sin,
                )
        return carry

    lax.fori_loop(0, 32, step, 0)


def beam_weights(upper, codes, flags):
    stations = codes.shape[1]
    codes = jnp.repeat(codes, 2, axis=1)
    scale = flags.astype(F32) / jnp.sqrt(jnp.float32(stations))
    scale = jnp.repeat(scale, 2)[None, :]
    return pl.pallas_call(
        weights_body,
        out_shape=jax.ShapeDtypeStruct((RADIX_A, 128, 2 * stations), BF16),
        in_specs=[
            pl.BlockSpec(memory_space=pltpu.SMEM),
            pl.BlockSpec(memory_space=pltpu.VMEM),
            pl.BlockSpec(memory_space=pltpu.VMEM),
        ],
        out_specs=pl.BlockSpec(memory_space=pltpu.VMEM),
        compiler_params=pltpu.CompilerParams(vmem_limit_bytes=VMEM_LIMIT),
        cost_estimate=pl.CostEstimate(
            flops=8 * RADIX_A * 128 * 2 * stations,
            bytes_accessed=2 * RADIX_A * 128 * 2 * stations,
            transcendentals=0,
        ),
    )(upper, codes, scale)


def beams_body(quads, held, last, x_ref, w_ref, *refs):
    if last:
        early_ref, out_ref, total = refs
    else:
        out_ref, = refs
        total = None
    lane = lax.broadcasted_iota(jnp.int32, (1, 128), 1)
    for group in range(quads):
        low = group * 128 // (16 * quads)
        data = x_ref[:, group].reshape(8 * 128, 128)
        picked = None
        for c in range(held):
            got = jnp.dot(w_ref[4 * low + c], data, preferred_element_type=F32)
            where = group * 128 + lane
            c1 = where // (16 * quads) * 4 + where % 16 // 4
            picked = jnp.where(c1 == 4 * low + c, got, 0.0 if picked is None else picked)
        turned = picked.T
        for m in range(0, 128, 4):
            at = group * 128 + m
            c1 = at // (16 * quads) * 4 + at % 16 // 4
            q = at % (16 * quads) // 16
            pol = q // (quads // 2)
            t = q % (quads // 2) * QUAD
            piece = turned[m : m + 4]
            if last:
                total[c1, pol, t : t + QUAD, :] = piece
            else:
                out_ref[c1, pol, t : t + QUAD, :] = piece
    if last:
        spectra = total.shape[2]
        early = early_ref.shape[2]
        for c1 in range(RADIX_A):
            for pol in range(2):
                total[c1, pol, spectra - early :, :] = early_ref[c1, pol]
        out_ref[...] = total[...].astype(BF16)


def beams(received, weights, quads, early):
    count = quads * QUAD // 2
    held = 4 * max(
        (g * 128 + 127) // (16 * quads) - g * 128 // (16 * quads) + 1 for g in range(quads)
    )
    received = received.reshape(RADIX_B, quads, 8, 128)
    operands = [received, weights]
    last = early is not None
    scratch = []
    if last:
        operands.append(early)
        spectra = count + early.shape[2]
        out_shape = jax.ShapeDtypeStruct((RADIX_A, 2, spectra, 128), BF16)
        scratch = [pltpu.VMEM((RADIX_A, 2, spectra, 128), F32)]
    else:
        out_shape = jax.ShapeDtypeStruct((RADIX_A, 2, count, 128), F32)
    return pl.pallas_call(
        functools.partial(beams_body, quads, held, last),
        out_shape=out_shape,
        in_specs=[pl.BlockSpec(memory_space=pltpu.VMEM)] * len(operands),
        out_specs=pl.BlockSpec(memory_space=pltpu.VMEM),
        scratch_shapes=scratch,
        compiler_params=pltpu.CompilerParams(vmem_limit_bytes=VMEM_LIMIT),
        cost_estimate=pl.CostEstimate(
            flops=2 * quads * held * 128 * 1024 * 128,
            bytes_accessed=2 * weights.size + 2 * received.size,
            transcendentals=0,
        ),
    )(*operands)


def turn(spectra):
    spectra = spectra.reshape(RADIX_B, -1, 128)
    return lax.all_to_all(spectra, "stn", split_axis=0, concat_axis=0, tiled=True)


def shards(samples, taps, codes, flags):
    stations = samples.shape[0]
    frames = samples.shape[3] // LENGTH
    size = lax.axis_size("tm")
    x = samples.reshape(stations, 2, 2, frames * RADIX_A, RADIX_B)
    x = x.transpose(0, 1, 3, 2, 4).reshape(stations, 2, frames * ROWS, RADIX_B)
    history = x[:, :, (frames - TAPS + 1) * ROWS :]
    halo = lax.ppermute(history, "tm", [(i, i + 1) for i in range(size - 1)])

    tables = (jnp.asarray(outer_table()), jnp.asarray(twiddles()), jnp.asarray(inner_table()))
    late = frames - QUAD
    early_sent = channelise(x, None, taps, tables, late, QUAD)
    early_got = turn(early_sent)
    upper = lax.axis_index("stn").astype(jnp.int32).reshape(1)
    weights = beam_weights(upper, codes, flags)
    main_sent = channelise(x, halo, taps, tables, 0, late)
    main_got = turn(main_sent)
    early = beams(early_got, weights, 2, None)
    return beams(main_got, weights, 2 * late // QUAD, early)


def solution(mesh):
    in_specs = (P("stn", None, None, "tm"), P(), P(), P())
    out_specs = P("stn", None, "tm", None)
    return jax.shard_map(shards, mesh=mesh, in_specs=in_specs, out_specs=out_specs, check_vma=False)
```

```python
import functools

import jax
import jax.numpy as jnp
import ml_dtypes
import numpy as np
from jax import lax
from jax.experimental import pallas as pl
from jax.experimental.pallas import tpu as pltpu
from jax.sharding import PartitionSpec as P

RADIX_A = 32
RADIX_B = 128
TAPS = 12
LENGTH = RADIX_A * RADIX_B
ROWS = 2 * RADIX_A
QUAD = 4
BF16 = jnp.bfloat16
F32 = jnp.float32
VMEM_LIMIT = 20 << 20


def params():
    return pltpu.CompilerParams(vmem_limit_bytes=VMEM_LIMIT)


def in_hbm(array):
    return pltpu.with_memory_space_constraint(array, pltpu.HBM)


IN_VMEM = pl.BlockSpec(memory_space=pltpu.VMEM)
IN_HBM = pl.BlockSpec(memory_space=pltpu.HBM)
LIGHT = pl.CostEstimate(flops=1024, bytes_accessed=1024, transcendentals=0)


def dft_table(radix):
    indices = np.arange(radix)
    angles = (indices[:, None] * indices[None, :] % radix) * (2.0 * np.pi / radix)
    cosine = np.cos(angles).astype(ml_dtypes.bfloat16)
    sine = np.sin(angles).astype(ml_dtypes.bfloat16)
    return np.stack(
        [np.stack([cosine, -sine], axis=1), np.stack([sine, cosine], axis=1)], axis=0
    )


def outer_table():
    table = dft_table(RADIX_A)
    grid = np.zeros((2, RADIX_A, QUAD, QUAD, RADIX_A, 2), ml_dtypes.bfloat16)
    for i in range(QUAD):
        grid[:, :, i, i] = table.transpose(2, 3, 1, 0)
    return grid.reshape(2 * RADIX_A * QUAD, QUAD * ROWS)


def inner_table():
    return dft_table(RADIX_B).reshape(2 * RADIX_B, 2 * RADIX_B).T.copy()


def twiddles():
    c1 = np.repeat(np.arange(RADIX_A), QUAD)
    angles = (c1[:, None] * np.arange(RADIX_B)[None, :] % LENGTH) * (2.0 * np.pi / LENGTH)
    scale = 1.0 / np.sqrt(np.float64(LENGTH))
    return np.stack([np.cos(angles) * scale, np.sin(angles) * scale]).astype(np.float32)


def spread_taps(taps_ref, taps2):
    for a in range(RADIX_A):
        for k in range(TAPS):
            row = taps_ref[k : k + 1, a * RADIX_B : (a + 1) * RADIX_B]
            taps2[k, 2 * a : 2 * a + 2, :] = jnp.broadcast_to(row, (2, RADIX_B))


def fir(first, count, base, stations, x_ref, halo_ref, taps2, filt):
    pieces = ROWS // 16

    def step(at, carry):
        station = at // (2 * pieces)
        pol = at // pieces % 2
        row = pl.multiple_of(at % pieces * 16, 16)
        frames = []
        for f in range(first - TAPS + 1, first + count):
            if f < 0:
                where = pl.multiple_of((f + TAPS - 1) * ROWS + row, 16)
                piece = halo_ref[station, pol, pl.ds(where, 16), :]
            else:
                where = pl.multiple_of(f * ROWS + row, 16)
                piece = x_ref[base + station, pol, pl.ds(where, 16), :]
            frames.append(piece.astype(F32))
        taps = [taps2[k, pl.ds(row, 16), :] for k in range(TAPS)]
        halves = []
        for half in range(2):
            rows = slice(8 * half, 8 * half + 8)
            outs = []
            for t in range(count):
                total = taps[0][rows] * frames[t][rows]
                for k in range(1, TAPS):
                    total = total + taps[k][rows] * frames[t + k][rows]
                outs.append(total)
            halves.append(outs)
        for t in range(count):
            both = jnp.concatenate([halves[0][t], halves[1][t]], axis=0).astype(BF16)
            where = pl.multiple_of(((station * 2 + pol) * count + t) * ROWS + row, 16)
            filt[pl.ds(where, 16), :] = both
        return carry

    lax.fori_loop(0, stations * 2 * pieces, step, 0)


def outer_stage(quads, stations, base, filt, outer_ref, tw_ref, mid):
    half = RADIX_A * QUAD
    size = QUAD * ROWS
    cosine = tw_ref[0]
    sine = tw_ref[1]
    table = outer_ref[...]
    for s in range(stations):
        for pair in range(quads // 2):
            at = (s * quads + 2 * pair) * size
            data = jnp.concatenate([filt[at : at + size, :], filt[at + size : at + 2 * size, :]], axis=1)
            got = jnp.dot(table, data, preferred_element_type=F32)
            for side in range(2):
                q = 2 * pair + side
                real = got[:half, side * 128 : side * 128 + 128]
                imag = got[half:, side * 128 : side * 128 + 128]
                real_out = (real * cosine + imag * sine).astype(BF16)
                imag_out = (imag * cosine - real * sine).astype(BF16)
                for g in range(half // 16):
                    to = ((base + s) * half // 16 * quads + g * quads + q) * 16
                    mid[to : to + 16, :RADIX_B] = real_out[16 * g : 16 * g + 16]
                    mid[to : to + 16, RADIX_B:] = imag_out[16 * g : 16 * g + 16]


def inner_stage(quads, station, data_ref, start, inner_ref, turn):
    block = 8 * quads
    for pair in range(quads // 2):
        at = start + pair * 256
        got = lax.dot_general(
            inner_ref[...],
            data_ref[at : at + 256, :],
            (((1,), (1,)), ((), ())),
            preferred_element_type=F32,
        )
        for side in range(2):
            group = 2 * pair + side
            for part in range(2):
                for c in range(0, RADIX_B, 8):
                    to = c * block + group * 8 + part + 2 * station
                    turn[pl.ds(to, 8, stride=block), :] = got[
                        part * RADIX_B + c : part * RADIX_B + c + 8,
                        side * 128 : side * 128 + 128,
                    ]


def send_out(turn, packed, out_ref, sems):
    rows = turn.shape[0]
    parts = sems.shape[0]
    size = rows // parts
    copies = []
    for p in range(parts):
        packed[p * size : (p + 1) * size, :] = turn[p * size : (p + 1) * size, :].astype(BF16)
        copy = pltpu.make_async_copy(
            packed.at[pl.ds(p * size, size)], out_ref.at[pl.ds(p * size, size)], sems.at[p]
        )
        copy.start()
        copies.append(copy)
    for copy in copies:
        copy.wait()


def early_body(
    first, count, quads, stations, x_hbm, taps_hbm, outer_hbm, tw_hbm, inner_hbm,
    out_ref, taps2, x_ref, taps_ref, outer_ref, tw_ref, inner_ref, filt, mid, turn, packed, sems, in_sems,
):
    pairs = [(taps_hbm, taps_ref)]
    pairs += [(x_hbm.at[s], x_ref.at[s]) for s in range(stations)]
    pairs += [(outer_hbm, outer_ref), (tw_hbm, tw_ref), (inner_hbm, inner_ref)]
    copies = [pltpu.make_async_copy(a, b, in_sems.at[i]) for i, (a, b) in enumerate(pairs)]
    for copy in copies:
        copy.start()
    copies[0].wait()
    spread_taps(taps_ref, taps2)
    for s in range(stations):
        copies[1 + s].wait()
    fir(first, count, 0, stations, x_ref, None, taps2, filt)
    for copy in copies[1 + stations :]:
        copy.wait()
    outer_stage(quads, stations, 0, filt, outer_ref, tw_ref, mid)
    for s in range(stations):
        inner_stage(quads, s, mid, s * 128 * quads, inner_ref, turn)
    send_out(turn, packed, out_ref, sems)


def half_body(count, quads, stations, x_ref, halo_ref, taps2, outer_ref, tw_ref, mid_ref, filt):
    fir(0, count, 0, stations, x_ref, halo_ref, taps2, filt)
    outer_stage(quads, stations, 0, filt, outer_ref, tw_ref, mid_ref)


def rest_body(
    count, quads, base, stations, x_ref, halo_ref, taps2, outer_ref, tw_ref, inner_ref, before_ref,
    out_ref, filt, mid, turn, packed, sems,
):
    fir(0, count, base, stations, x_ref, halo_ref, taps2, filt)
    for s in range(base):
        inner_stage(quads, s, before_ref, s * 128 * quads, inner_ref, turn)
    outer_stage(quads, stations, 0, filt, outer_ref, tw_ref, mid)
    for s in range(stations):
        inner_stage(quads, base + s, mid, s * 128 * quads, inner_ref, turn)
    send_out(turn, packed, out_ref, sems)


def channelise_early(x, taps, outer, tw, inner, first, count):
    stations = x.shape[0]
    quads = 2 * count // QUAD
    rows = RADIX_B * 8 * quads
    return pl.pallas_call(
        functools.partial(early_body, first, count, quads, stations),
        out_shape=(
            pltpu.HBM((rows, 128), BF16),
            jax.ShapeDtypeStruct((TAPS, ROWS, RADIX_B), F32),
        ),
        in_specs=[IN_HBM] * 5,
        out_specs=(IN_HBM, IN_VMEM),
        scratch_shapes=[
            pltpu.VMEM(x.shape, BF16),
            pltpu.VMEM(taps.shape, F32),
            pltpu.VMEM(outer.shape, BF16),
            pltpu.VMEM(tw.shape, F32),
            pltpu.VMEM(inner.shape, BF16),
            pltpu.VMEM((stations * 2 * count * ROWS, RADIX_B), BF16),
            pltpu.VMEM((stations * 128 * quads, 2 * RADIX_B), BF16),
            pltpu.VMEM((rows, 128), F32),
            pltpu.VMEM((rows, 128), BF16),
            pltpu.SemaphoreType.DMA((4,)),
            pltpu.SemaphoreType.DMA((stations + 4,)),
        ],
        compiler_params=params(),
        cost_estimate=LIGHT,
    )(*map(in_hbm, (x, taps, outer, tw, inner)))


def channelise_half(x, halo, taps2, outer, tw, count):
    stations = halo.shape[0]
    quads = 2 * count // QUAD
    return pl.pallas_call(
        functools.partial(half_body, count, quads, stations),
        out_shape=jax.ShapeDtypeStruct((stations * 128 * quads, 2 * RADIX_B), BF16),
        in_specs=[IN_VMEM] * 5,
        out_specs=IN_VMEM,
        scratch_shapes=[pltpu.VMEM((stations * 2 * count * ROWS, RADIX_B), BF16)],
        compiler_params=params(),
        cost_estimate=LIGHT,
    )(x, halo, taps2, outer, tw)


def channelise_rest(x, halo, taps2, outer, tw, inner, before, count):
    stations = halo.shape[0]
    base = x.shape[0] - stations
    quads = 2 * count // QUAD
    rows = RADIX_B * 8 * quads
    return pl.pallas_call(
        functools.partial(rest_body, count, quads, base, stations),
        out_shape=pltpu.HBM((rows, 128), BF16),
        in_specs=[IN_VMEM] * 7,
        out_specs=IN_HBM,
        scratch_shapes=[
            pltpu.VMEM((stations * 2 * count * ROWS, RADIX_B), BF16),
            pltpu.VMEM((stations * 128 * quads, 2 * RADIX_B), BF16),
            pltpu.VMEM((rows, 128), F32),
            pltpu.VMEM((rows, 128), BF16),
            pltpu.SemaphoreType.DMA((8,)),
        ],
        compiler_params=params(),
        cost_estimate=LIGHT,
    )(x, halo, taps2, outer, tw, inner, before)


def history_body(station, start, x_ref, out_ref, sems):
    copies = []
    for s in range(out_ref.shape[0]):
        for pol in range(2):
            copy = pltpu.make_async_copy(
                x_ref.at[station + s, pol, pl.ds(start, out_ref.shape[2])],
                out_ref.at[s, pol],
                sems.at[2 * s + pol],
            )
            copy.start()
            copies.append(copy)
    for copy in copies:
        copy.wait()


def history(x, frames, station, stations):
    rows = frames * ROWS
    return pl.pallas_call(
        functools.partial(history_body, station, x.shape[2] - rows),
        out_shape=pltpu.VMEM((stations, 2, rows, RADIX_B), BF16),
        in_specs=[IN_HBM],
        out_specs=IN_VMEM,
        scratch_shapes=[pltpu.SemaphoreType.DMA((2 * stations,))],
        compiler_params=params(),
        cost_estimate=LIGHT,
    )(in_hbm(x))


def weights_body(upper_ref, codes_ref, scale_ref, hbm_ref, out_ref, sem):
    upper = upper_ref[0]
    unit = 2.0 * np.pi / LENGTH

    def step(at, carry):
        row = pl.multiple_of(at // 8 * 16, 16)
        col = pl.multiple_of(at % 8 * 128, 128)
        codes = codes_ref[pl.ds(row, 16), pl.ds(col, 128)]
        scale = scale_ref[:, pl.ds(col, 128)]
        start = ((codes * (upper * RADIX_A)) & (LENGTH - 1)).astype(F32) * unit
        by = codes.astype(F32) * unit
        odd = (lax.broadcasted_iota(jnp.int32, (16, 128), 1) & 1) == 1
        cosine = jnp.cos(start) * scale
        sine = jnp.sin(start) * scale
        here = jnp.where(odd, sine, cosine)
        across = jnp.where(odd, cosine, -sine)
        by_cos = jnp.cos(by)
        by_sin = jnp.sin(by)
        for c1 in range(RADIX_A):
            out_ref[c1, pl.ds(row, 16), pl.ds(col, 128)] = here.astype(BF16)
            if c1 + 1 < RADIX_A:
                here, across = here * by_cos + across * by_sin, across * by_cos - here * by_sin
        return carry

    lax.fori_loop(0, 32, step, 0)
    copy = pltpu.make_async_copy(out_ref, hbm_ref, sem)
    copy.start()
    copy.wait()


def beam_weights(upper, codes, flags):
    beam_count, stations = codes.shape
    codes = jnp.repeat(codes, 2, axis=1)
    scale = flags.astype(F32) / jnp.sqrt(jnp.float32(stations))
    scale = jnp.repeat(scale, 2)[None, :]
    shape = (RADIX_A, beam_count, 2 * stations)
    return pl.pallas_call(
        weights_body,
        out_shape=pltpu.HBM(shape, BF16),
        in_specs=[pl.BlockSpec(memory_space=pltpu.SMEM), IN_VMEM, IN_VMEM],
        out_specs=IN_HBM,
        scratch_shapes=[pltpu.VMEM(shape, BF16), pltpu.SemaphoreType.DMA],
        compiler_params=params(),
        cost_estimate=LIGHT,
    )(upper, codes, scale)


def beams_body(quads, last, x_ref, w_hbm, *refs):
    if last:
        early_ref, out_ref, total, w_ref, sems = refs
    else:
        out_ref, w_ref, sems = refs
        total = out_ref
    copies = []
    for g in range(RADIX_A // 4):
        part = pl.ds(4 * g, 4)
        copies.append(pltpu.make_async_copy(w_hbm.at[part], w_ref.at[part], sems.at[g]))
        copies[g].start()
    waited = 0
    beam_count = w_ref.shape[1]
    lane = lax.broadcasted_iota(jnp.int32, (1, 128), 1)
    even = (lax.broadcasted_iota(jnp.int32, (1, 8, 128), 1) & 1) == 0
    for group in range(quads):
        base = group * 128
        low = base // (16 * quads)
        high = (base + 127) // (16 * quads)
        values = x_ref[:, group]
        wide = values.astype(F32)
        swapped = jnp.where(even, pltpu.roll(wide, 7, 1), -pltpu.roll(wide, 1, 1)).astype(BF16)
        data = jnp.concatenate([values.reshape(1024, 128), swapped.reshape(1024, 128)], axis=1)
        c1 = (base + lane) // (16 * quads) * 4 + lane % 16 // 4
        real = imag = None
        for g in range(low, high + 1):
            while waited <= g:
                copies[waited].wait()
                waited += 1
            weights = w_ref[4 * g : 4 * g + 4].reshape(4 * beam_count, 1024)
            got = jnp.dot(weights, data, preferred_element_type=F32)
            for c in range(4):
                piece = got[beam_count * c : beam_count * (c + 1)]
                if real is None:
                    real, imag = piece[:, :128], piece[:, 128:]
                else:
                    mine = c1 == 4 * g + c
                    real = jnp.where(mine, piece[:, :128], real)
                    imag = jnp.where(mine, piece[:, 128:], imag)
        turned = jnp.concatenate([real, imag], axis=0).T
        for m in range(0, 128, 4):
            at = base + m
            channel = at // (16 * quads) * 4 + at % 16 // 4
            q = at % (16 * quads) // 16
            pol = q // (quads // 2)
            t = q % (quads // 2) * QUAD
            total[channel, pol, t : t + QUAD, :] = turned[m : m + 4]
    if last:
        spectra = total.shape[2]
        early = early_ref.shape[2]
        for channel in range(RADIX_A):
            for pol in range(2):
                total[channel, pol, spectra - early :, :] = early_ref[channel, pol]
        out_ref[...] = total[...].astype(BF16)


def beams(received, weights, quads, early):
    count = quads * QUAD // 2
    received = received.reshape(RADIX_B, quads, 8, 128)
    operands = [received, in_hbm(weights)]
    in_specs = [IN_VMEM, IN_HBM]
    scratch = [pltpu.VMEM(weights.shape, BF16), pltpu.SemaphoreType.DMA((RADIX_A // 4,))]
    last = early is not None
    if last:
        operands.append(early)
        in_specs.append(IN_VMEM)
        shape = (RADIX_A, 2, count + early.shape[2], 128)
        out_shape = jax.ShapeDtypeStruct(shape, BF16)
        scratch = [pltpu.VMEM(shape, F32)] + scratch
    else:
        out_shape = jax.ShapeDtypeStruct((RADIX_A, 2, count, 128), F32)
    return pl.pallas_call(
        functools.partial(beams_body, quads, last),
        out_shape=out_shape,
        in_specs=in_specs,
        out_specs=IN_VMEM,
        scratch_shapes=scratch,
        compiler_params=params(),
        cost_estimate=LIGHT,
    )(*operands)


def turn(spectra):
    spectra = spectra.reshape(RADIX_B, -1, 128)
    return lax.all_to_all(spectra, "stn", split_axis=0, concat_axis=0, tiled=True)


def shards(samples, taps, codes, flags):
    stations = samples.shape[0]
    frames = samples.shape[3] // LENGTH
    size = lax.axis_size("tm")
    x = samples.reshape(stations, 2, 2, frames * RADIX_A, RADIX_B)
    x = x.transpose(0, 1, 3, 2, 4).reshape(stations, 2, frames * ROWS, RADIX_B)
    pairs = [(i, i + 1) for i in range(size - 1)]
    halos = [
        lax.ppermute(history(x, TAPS - 1, station, count), "tm", pairs)
        for station, count in ((0, stations - 1), (stations - 1, 1))
    ]

    outer, tw, inner = jnp.asarray(outer_table()), jnp.asarray(twiddles()), jnp.asarray(inner_table())
    late = frames - QUAD
    early_sent, taps2 = channelise_early(x, taps, outer, tw, inner, late, QUAD)
    early_got = turn(early_sent)
    upper = lax.axis_index("stn").astype(jnp.int32).reshape(1)
    weights = beam_weights(upper, codes, flags)
    before = channelise_half(x, halos[0], taps2, outer, tw, late)
    main_sent = channelise_rest(x, halos[1], taps2, outer, tw, inner, before, late)
    main_got = turn(main_sent)
    early = beams(early_got, weights, 2, None)
    return beams(main_got, weights, 2 * late // QUAD, early)


def solution(mesh):
    in_specs = (P("stn", None, None, "tm"), P(), P(), P())
    out_specs = P("stn", None, "tm", None)
    return jax.shard_map(shards, mesh=mesh, in_specs=in_specs, out_specs=out_specs, check_vma=False)
```

```python
import functools

import jax
import jax.numpy as jnp
import ml_dtypes
import numpy as np
from jax import lax
from jax.experimental import pallas as pl
from jax.experimental.pallas import tpu as pltpu
from jax.sharding import PartitionSpec as P

RADIX_A = 32
RADIX_B = 128
TAPS = 12
LENGTH = RADIX_A * RADIX_B
ROWS = 2 * RADIX_A
PAIR = 2
QUAD = 2 * PAIR
EARLY = 6
BF16 = jnp.bfloat16
F32 = jnp.float32
VMEM_LIMIT = 16 << 20


def params():
    return pltpu.CompilerParams(vmem_limit_bytes=VMEM_LIMIT)


def in_hbm(array):
    return pltpu.with_memory_space_constraint(array, pltpu.HBM)


IN_VMEM = pl.BlockSpec(memory_space=pltpu.VMEM)
IN_HBM = pl.BlockSpec(memory_space=pltpu.HBM)
LIGHT = pl.CostEstimate(flops=1024, bytes_accessed=1024, transcendentals=0)
HEAVY = pl.CostEstimate(flops=1 << 37, bytes_accessed=1024, transcendentals=0)


def dft_table(radix):
    indices = np.arange(radix)
    angles = (indices[:, None] * indices[None, :] % radix) * (2.0 * np.pi / radix)
    cosine = np.cos(angles).astype(ml_dtypes.bfloat16)
    sine = np.sin(angles).astype(ml_dtypes.bfloat16)
    return np.stack(
        [np.stack([cosine, -sine], axis=1), np.stack([sine, cosine], axis=1)], axis=0
    )


def outer_table():
    table = dft_table(RADIX_A).transpose(2, 3, 1, 0)
    table = table.reshape(2, RADIX_A // 4, 4, RADIX_A, 2)
    grid = np.zeros((2, RADIX_A // 4, PAIR, 4, 2, 2, PAIR, RADIX_A, 2), ml_dtypes.bfloat16)
    for spectrum in range(PAIR):
        for pol in range(2):
            grid[:, :, spectrum, :, pol, pol, spectrum] = table
    return grid.reshape(2 * RADIX_A * QUAD, QUAD * ROWS)


def inner_table():
    return dft_table(RADIX_B).reshape(2 * RADIX_B, 2 * RADIX_B).T.copy()


def twiddles():
    c1 = np.zeros((RADIX_A // 4, PAIR, 4, 2), np.int64)
    c1 += np.arange(RADIX_A).reshape(RADIX_A // 4, 1, 4, 1)
    angles = (c1.reshape(-1, 1) * np.arange(RADIX_B) % LENGTH) * (2.0 * np.pi / LENGTH)
    scale = 1.0 / np.sqrt(np.float64(LENGTH))
    return np.stack([np.cos(angles) * scale, np.sin(angles) * scale]).astype(np.float32)


def spread_taps(taps_ref, taps2):
    for a in range(RADIX_A):
        for k in range(TAPS):
            row = taps_ref[k : k + 1, a * RADIX_B : (a + 1) * RADIX_B]
            taps2[k, 2 * a : 2 * a + 2, :] = jnp.broadcast_to(row, (2, RADIX_B))


def fir(first, count, base, stations, x_ref, near_ref, far_ref, taps2, filt, place):
    pieces = ROWS // 16

    def step(at, carry):
        station = at // (2 * pieces)
        pol = at // pieces % 2
        row = pl.multiple_of(at % pieces * 16, 16)
        frames = []
        for f in range(first - TAPS + 1, first + count):
            if f < -1:
                where = pl.multiple_of((f + TAPS - 1) * ROWS + row, 16)
                piece = far_ref[station, pol, pl.ds(where, 16), :]
            elif f < 0:
                piece = near_ref[base + station, pol, pl.ds(row, 16), :]
            else:
                where = pl.multiple_of(f * ROWS + row, 16)
                piece = x_ref[base + station, pol, pl.ds(where, 16), :]
            frames.append(piece.astype(F32))
        taps = [taps2[k, pl.ds(row, 16), :] for k in range(TAPS)]
        halves = []
        for half in range(2):
            rows = slice(8 * half, 8 * half + 8)
            outs = []
            for t in range(count):
                total = taps[0][rows] * frames[t][rows]
                for k in range(1, TAPS):
                    total = total + taps[k][rows] * frames[t + k][rows]
                outs.append(total)
            halves.append(outs)
        for t in range(count):
            both = jnp.concatenate([halves[0][t], halves[1][t]], axis=0).astype(BF16)
            where = pl.multiple_of(place(station, pol, t) * ROWS + row, 16)
            filt[pl.ds(where, 16), :] = both
        return carry

    lax.fori_loop(0, stations * 2 * pieces, step, 0)


def outer_stage(quads, stations, frame, outer_ref, tw_ref, mid):
    half = RADIX_A * QUAD
    cosine = tw_ref[0]
    sine = tw_ref[1]
    table = outer_ref[...]
    for first in range(0, stations * quads, 2):
        held = range(first, min(first + 2, stations * quads))
        data = []
        for n in held:
            s, q = n // quads, n % quads
            data.append([frame(s, pol, PAIR * q + t) for pol in range(2) for t in range(PAIR)])
        data = jnp.concatenate([jnp.concatenate(frames, axis=0) for frames in data], axis=1)
        got = jnp.dot(table, data, preferred_element_type=F32)
        for side, n in enumerate(held):
            s, q = n // quads, n % quads
            real = got[:half, side * 128 : side * 128 + 128]
            imag = got[half:, side * 128 : side * 128 + 128]
            real_out = (real * cosine + imag * sine).astype(BF16)
            imag_out = (imag * cosine - real * sine).astype(BF16)
            for g in range(half // 16):
                to = (s * half // 16 * quads + g * quads + q) * 16
                mid[to : to + 16, :RADIX_B] = real_out[16 * g : 16 * g + 16]
                mid[to : to + 16, RADIX_B:] = imag_out[16 * g : 16 * g + 16]


def inner_stage(quads, station, data_ref, start, inner_ref, turn):
    block = 8 * quads
    for first in range(0, quads, 2):
        wide = min(2, quads - first)
        at = start + first * 128
        got = lax.dot_general(
            inner_ref[...],
            data_ref[at : at + wide * 128, :],
            (((1,), (1,)), ((), ())),
            preferred_element_type=F32,
        )
        for side in range(wide):
            group = first + side
            for part in range(2):
                for c in range(0, RADIX_B, 8):
                    to = c * block + group * 8 + part + 2 * station
                    turn[pl.ds(to, 8, stride=block), :] = got[
                        part * RADIX_B + c : part * RADIX_B + c + 8,
                        side * 128 : side * 128 + 128,
                    ]


def send_out(turn, packed, out_ref, sems, before=None, station=0):
    rows = turn.shape[0]
    parts = sems.shape[0]
    size = rows // parts
    own = lax.broadcasted_iota(jnp.int32, (size, 128), 0) % 8 >= 2 * station
    copies = []
    for p in range(parts):
        part = pl.ds(p * size, size)
        values = turn[part, :]
        if before is not None:
            values = jnp.where(own, values, before[part, :])
        packed[part, :] = values.astype(BF16)
        copy = pltpu.make_async_copy(packed.at[part], out_ref.at[part], sems.at[p])
        copy.start()
        copies.append(copy)
    for copy in copies:
        copy.wait()


def fetch(pairs, sems):
    copies = [pltpu.make_async_copy(a, b, sems.at[i]) for i, (a, b) in enumerate(pairs)]
    for copy in copies:
        copy.start()
    return copies


def rows_of(filt, block):
    return filt[block * ROWS : (block + 1) * ROWS, :]


def first_body(first, count, stations, x_ref, taps2, filt):
    fir(first, count, 0, stations, x_ref, None, None, taps2, filt, lambda s, pol, t: (s * 2 + pol) * count + t)


def early_body(
    first, count, quads, stations, x_ref, near_ref, taps2, before, outer_hbm, tw_hbm, inner_hbm, out_ref,
    outer_ref, tw_ref, inner_ref, filt, mid, turn, packed, sems, in_sems,
):
    copies = fetch([(outer_hbm, outer_ref), (tw_hbm, tw_ref), (inner_hbm, inner_ref)], in_sems)
    fir(first, 1, 0, stations, x_ref, near_ref, None, taps2, filt, lambda s, pol, t: s * 2 + pol)
    for copy in copies:
        copy.wait()

    def frame(s, pol, t):
        if t == 0:
            return rows_of(filt, s * 2 + pol)
        return rows_of(before, (s * 2 + pol) * (count - 1) + t - 1)

    outer_stage(quads, stations, frame, outer_ref, tw_ref, mid)
    for s in range(stations):
        inner_stage(quads, s, mid, s * 128 * quads, inner_ref, turn)
    send_out(turn, packed, out_ref, sems)


def late_body(
    last, count, quads, base, stations, x_ref, near_ref, far_ref, taps2, outer_hbm, tw_hbm, inner_hbm, *refs
):
    if last:
        before, out_ref, outer_ref, tw_ref, inner_ref, filt, mid, in_sems, turn, packed, sems = refs
    else:
        turn, outer_ref, tw_ref, inner_ref, filt, mid, in_sems = refs

    def place(s, pol, t):
        return (s * 2 + pol) * count + t

    copies = fetch([(outer_hbm, outer_ref), (tw_hbm, tw_ref), (inner_hbm, inner_ref)], in_sems)
    fir(0, count, base, stations, x_ref, near_ref, far_ref, taps2, filt, place)
    for copy in copies:
        copy.wait()
    outer_stage(quads, stations, lambda *at: rows_of(filt, place(*at)), outer_ref, tw_ref, mid)
    for s in range(stations):
        inner_stage(quads, base + s, mid, s * 128 * quads, inner_ref, turn)
    if last:
        send_out(turn, packed, out_ref, sems, before, base)


def filter_first(x, taps2, first, count):
    stations = x.shape[0]
    return pl.pallas_call(
        functools.partial(first_body, first, count, stations),
        out_shape=jax.ShapeDtypeStruct((stations * 2 * count * ROWS, RADIX_B), BF16),
        in_specs=[IN_VMEM, IN_VMEM],
        out_specs=IN_VMEM,
        compiler_params=params(),
        cost_estimate=LIGHT,
    )(x, taps2)


def channelise_early(x, near, taps2, before, tables, first, count):
    stations = x.shape[0]
    quads = 2 * count // QUAD
    rows = RADIX_B * 8 * quads
    return pl.pallas_call(
        functools.partial(early_body, first, count, quads, stations),
        out_shape=pltpu.HBM((rows, 128), BF16),
        in_specs=[IN_VMEM] * 4 + [IN_HBM] * 3,
        out_specs=IN_HBM,
        scratch_shapes=[pltpu.VMEM(table.shape, table.dtype) for table in tables]
        + [
            pltpu.VMEM((stations * 2 * ROWS, RADIX_B), BF16),
            pltpu.VMEM((stations * 128 * quads, 2 * RADIX_B), BF16),
            pltpu.VMEM((rows, 128), F32),
            pltpu.VMEM((rows, 128), BF16),
            pltpu.SemaphoreType.DMA((4,)),
            pltpu.SemaphoreType.DMA((3,)),
        ],
        compiler_params=params(),
        cost_estimate=HEAVY,
    )(x, near, taps2, before, *map(in_hbm, tables))


def channelise_late(x, near, far, taps2, tables, base, count, before=None):
    stations = far.shape[0]
    quads = 2 * count // QUAD
    rows = RADIX_B * 8 * quads
    last = before is not None
    scratch = [pltpu.VMEM(table.shape, table.dtype) for table in tables] + [
        pltpu.VMEM((stations * 2 * count * ROWS, RADIX_B), BF16),
        pltpu.VMEM((stations * 128 * quads, 2 * RADIX_B), BF16),
        pltpu.SemaphoreType.DMA((3,)),
    ]
    if last:
        scratch += [
            pltpu.VMEM((rows, 128), F32),
            pltpu.VMEM((rows, 128), BF16),
            pltpu.SemaphoreType.DMA((8,)),
        ]
    return pl.pallas_call(
        functools.partial(late_body, last, count, quads, base, stations),
        out_shape=pltpu.HBM((rows, 128), BF16) if last else jax.ShapeDtypeStruct((rows, 128), F32),
        in_specs=[IN_VMEM] * 4 + [IN_HBM] * 3 + [IN_VMEM] * last,
        out_specs=IN_HBM if last else IN_VMEM,
        scratch_shapes=scratch,
        compiler_params=params(),
        cost_estimate=HEAVY,
    )(x, near, far, taps2, *map(in_hbm, tables), *([before] if last else []))


def history_body(starts, x_ref, *refs):
    count = len(starts)
    taps_ref = taps2 = None
    if len(refs) > 2 * count + 2:
        taps_hbm, refs = refs[0], refs[1:]
        taps2 = refs[count]
        refs = refs[:count] + refs[count + 1 :]
        taps_ref, taps_sem, refs = refs[-2], refs[-1], refs[:-2]
        taps_copy = pltpu.make_async_copy(taps_hbm, taps_ref, taps_sem)
        taps_copy.start()
    outs, helds, sems, out_sems = refs[:count], refs[count : 2 * count], refs[-2], refs[-1]
    pieces = []
    for (station, start), out, held in zip(starts, outs, helds):
        for s in range(out.shape[0]):
            at = len(pieces)
            source = x_ref.at[station + s, :, pl.ds(start, out.shape[2])]
            into = pltpu.make_async_copy(source, held.at[s], sems.at[at])
            onward = pltpu.make_async_copy(held.at[s], out.at[s], out_sems.at[at])
            into.start()
            pieces.append((into, onward))
    for into, onward in pieces:
        into.wait()
        onward.start()
    if taps_ref is not None:
        taps_copy.wait()
        spread_taps(taps_ref, taps2)
    for _, onward in pieces:
        onward.wait()


def history(x, parts, taps=None):
    shapes = [(n, 2, frames * ROWS, RADIX_B) for _, n, _, frames in parts]
    starts = [(station, frame * ROWS) for station, _, frame, _ in parts]
    pieces = sum(n for _, n, _, _ in parts)
    operands, in_specs, fetch = [in_hbm(x)], [IN_HBM], []
    out_shape = [pltpu.HBM(shape, BF16) for shape in shapes]
    out_specs = [IN_HBM] * len(parts)
    if taps is not None:
        operands.append(in_hbm(taps))
        in_specs.append(IN_HBM)
        fetch = [pltpu.VMEM(taps.shape, F32), pltpu.SemaphoreType.DMA]
        out_shape.append(jax.ShapeDtypeStruct((TAPS, ROWS, RADIX_B), F32))
        out_specs.append(IN_VMEM)
    return pl.pallas_call(
        functools.partial(history_body, starts),
        out_shape=out_shape,
        in_specs=in_specs,
        out_specs=out_specs,
        scratch_shapes=[pltpu.VMEM(shape, BF16) for shape in shapes]
        + [pltpu.SemaphoreType.DMA((pieces,))] * 2
        + fetch,
        compiler_params=params(),
        cost_estimate=LIGHT,
    )(*operands)


def weights_body(upper_ref, codes_ref, scale_ref, hbm_ref, out_ref, sem):
    upper = upper_ref[0]
    unit = 2.0 * np.pi / LENGTH

    def step(at, carry):
        row = pl.multiple_of(at // 8 * 16, 16)
        col = pl.multiple_of(at % 8 * 128, 128)
        codes = codes_ref[pl.ds(row, 16), pl.ds(col, 128)]
        scale = scale_ref[:, pl.ds(col, 128)]
        start = ((codes * (upper * RADIX_A)) & (LENGTH - 1)).astype(F32) * unit
        by = codes.astype(F32) * unit
        odd = (lax.broadcasted_iota(jnp.int32, (16, 128), 1) & 1) == 1
        cosine = jnp.cos(start) * scale
        sine = jnp.sin(start) * scale
        here = jnp.where(odd, sine, cosine)
        across = jnp.where(odd, cosine, -sine)
        by_cos = jnp.cos(by)
        by_sin = jnp.sin(by)
        for c1 in range(RADIX_A):
            out_ref[c1, pl.ds(row, 16), pl.ds(col, 128)] = here.astype(BF16)
            if c1 + 1 < RADIX_A:
                here, across = here * by_cos + across * by_sin, across * by_cos - here * by_sin
        return carry

    lax.fori_loop(0, 32, step, 0)
    copy = pltpu.make_async_copy(out_ref, hbm_ref, sem)
    copy.start()
    copy.wait()


def beam_weights(upper, codes, flags):
    beam_count, stations = codes.shape
    codes = jnp.repeat(codes, 2, axis=1)
    scale = flags.astype(F32) / jnp.sqrt(jnp.float32(stations))
    scale = jnp.repeat(scale, 2)[None, :]
    shape = (RADIX_A, beam_count, 2 * stations)
    return pl.pallas_call(
        weights_body,
        out_shape=pltpu.HBM(shape, BF16),
        in_specs=[pl.BlockSpec(memory_space=pltpu.SMEM), IN_VMEM, IN_VMEM],
        out_specs=IN_HBM,
        scratch_shapes=[pltpu.VMEM(shape, BF16), pltpu.SemaphoreType.DMA],
        compiler_params=params(),
        cost_estimate=LIGHT,
    )(upper, codes, scale)


def beams_body(quads, last, x_ref, w_hbm, *refs):
    if last:
        early_ref, out_ref, total, w_ref, sems = refs
    else:
        out_ref, w_ref, sems = refs
        total = out_ref
    copies = []
    for g in range(RADIX_A // 4):
        part = pl.ds(4 * g, 4)
        copies.append(pltpu.make_async_copy(w_hbm.at[part], w_ref.at[part], sems.at[g]))
        copies[g].start()
    waited = 0
    beam_count = w_ref.shape[1]
    spectra = total.shape[0] // (2 * RADIX_A)
    if last:
        early = early_ref.shape[0] // (2 * RADIX_A)
        for t in range(early):
            for row in range(0, 2 * RADIX_A, 8):
                total[pl.ds((row + 1) * spectra - early + t, 8, stride=spectra), :] = early_ref[
                    pl.ds(row * early + t, 8, stride=early), :
                ]
    lane = lax.broadcasted_iota(jnp.int32, (1, 128), 1)
    even = (lax.broadcasted_iota(jnp.int32, (1, 8, 128), 1) & 1) == 0
    for group in range(quads):
        base = group * 128
        low = base // (16 * quads)
        high = (base + 127) // (16 * quads)
        values = x_ref[:, group]
        wide = values.astype(F32)
        swapped = jnp.where(even, pltpu.roll(wide, 7, 1), -pltpu.roll(wide, 1, 1)).astype(BF16)
        data = jnp.concatenate([values.reshape(1024, 128), swapped.reshape(1024, 128)], axis=1)
        c1 = (base + lane) // (16 * quads) * 4 + lane % 8 // 2
        real = imag = None
        for g in range(low, high + 1):
            while waited <= g:
                copies[waited].wait()
                waited += 1
            weights = w_ref[4 * g : 4 * g + 4].reshape(4 * beam_count, 1024)
            got = jnp.dot(weights, data, preferred_element_type=F32)
            for c in range(4):
                piece = got[beam_count * c : beam_count * (c + 1)]
                if real is None:
                    real, imag = piece[:, :128], piece[:, 128:]
                else:
                    mine = c1 == 4 * g + c
                    real = jnp.where(mine, piece[:, :128], real)
                    imag = jnp.where(mine, piece[:, 128:], imag)
        turned = jnp.concatenate([real, imag], axis=0).T
        for m in range(0, 128, 8):
            at = base + m
            block = at // (16 * quads)
            t = at % (16 * quads) // 16 * PAIR + at % 16 // 8
            total[pl.ds(block * 8 * spectra + t, 8, stride=spectra), :] = turned[m : m + 8]
    if last:
        out_ref[...] = total[...].astype(BF16)


def beams(received, weights, quads, early):
    count = quads * QUAD // 2
    received = received.reshape(RADIX_B, quads, 8, 128)
    operands = [received, in_hbm(weights)]
    in_specs = [IN_VMEM, IN_HBM]
    scratch = [pltpu.VMEM(weights.shape, BF16), pltpu.SemaphoreType.DMA((RADIX_A // 4,))]
    last = early is not None
    if last:
        operands.append(early)
        in_specs.append(IN_VMEM)
        shape = (2 * RADIX_A * count + early.shape[0], 128)
        out_shape = jax.ShapeDtypeStruct(shape, BF16)
        scratch = [pltpu.VMEM(shape, F32)] + scratch
    else:
        out_shape = jax.ShapeDtypeStruct((2 * RADIX_A * count, 128), F32)
    return pl.pallas_call(
        functools.partial(beams_body, quads, last),
        out_shape=out_shape,
        in_specs=in_specs,
        out_specs=IN_VMEM,
        scratch_shapes=scratch,
        compiler_params=params(),
        cost_estimate=LIGHT,
    )(*operands)


def turn(spectra):
    spectra = spectra.reshape(RADIX_B, -1, 128)
    return lax.all_to_all(spectra, "stn", split_axis=0, concat_axis=0, tiled=True)


def shards(samples, taps, codes, flags):
    stations = samples.shape[0]
    frames = samples.shape[3] // LENGTH
    size = lax.axis_size("tm")
    x = samples.reshape(stations, 2, 2, frames * RADIX_A, RADIX_B)
    x = x.transpose(0, 1, 3, 2, 4).reshape(stations, 2, frames * ROWS, RADIX_B)
    pairs = [(i, i + 1) for i in range(size - 1)]
    lead = stations - 1
    rest = frames - TAPS + 1, TAPS - 2
    parts = [(0, stations, frames - 1, 1), (0, lead, *rest), (lead, 1, *rest)]
    near, far, far_last, taps2 = history(x, parts, taps)
    near = lax.ppermute(near, "tm", pairs)
    far = lax.ppermute(far, "tm", pairs)

    tables = (jnp.asarray(outer_table()), jnp.asarray(twiddles()), jnp.asarray(inner_table()))
    late = frames - EARLY
    filtered = filter_first(x, taps2, late + 1, EARLY - 1)
    early_sent = channelise_early(x, near, taps2, filtered, tables, late, EARLY)
    early_sent, far_last = lax.optimization_barrier((early_sent, far_last))
    early_got = turn(early_sent)
    far_last = lax.ppermute(far_last, "tm", pairs)
    upper = lax.axis_index("stn").astype(jnp.int32).reshape(1)
    weights = beam_weights(upper, codes, flags)
    ahead = channelise_late(x, near, far, taps2, tables, 0, late)
    main_sent = channelise_late(x, near, far_last, taps2, tables, lead, late, ahead)
    main_got = turn(main_sent)
    early = beams(early_got, weights, EARLY // PAIR, None)
    result = beams(main_got, weights, late // PAIR, early)
    return result.reshape(RADIX_A, 2, frames, 128)


def solution(mesh):
    in_specs = (P("stn", None, None, "tm"), P(), P(), P())
    out_specs = P("stn", None, "tm", None)
    return jax.shard_map(shards, mesh=mesh, in_specs=in_specs, out_specs=out_specs, check_vma=False)
```

```python
import functools

import jax
import jax.numpy as jnp
import ml_dtypes
import numpy as np
from jax import lax
from jax.experimental import pallas as pl
from jax.experimental.pallas import tpu as pltpu
from jax.sharding import PartitionSpec as P

RADIX_A = 32
RADIX_B = 128
TAPS = 12
LENGTH = RADIX_A * RADIX_B
ROWS = 2 * RADIX_A
PAIR = 2
QUAD = 2 * PAIR
KEPT = 16
NEAR = 1
EARLY = TAPS - 7 + NEAR
BF16 = jnp.bfloat16
F32 = jnp.float32
VMEM_LIMIT = 16 << 20


def params():
    return pltpu.CompilerParams(vmem_limit_bytes=VMEM_LIMIT)


def in_hbm(array):
    return pltpu.with_memory_space_constraint(array, pltpu.HBM)


IN_VMEM = pl.BlockSpec(memory_space=pltpu.VMEM)
IN_HBM = pl.BlockSpec(memory_space=pltpu.HBM)
LIGHT = pl.CostEstimate(flops=1024, bytes_accessed=1024, transcendentals=0)
SOME = pl.CostEstimate(flops=7 << 30, bytes_accessed=1024, transcendentals=0)
HEAVY = pl.CostEstimate(flops=1 << 37, bytes_accessed=1024, transcendentals=0)


def dft_table(radix):
    indices = np.arange(radix)
    angles = (indices[:, None] * indices[None, :] % radix) * (2.0 * np.pi / radix)
    cosine = np.cos(angles).astype(ml_dtypes.bfloat16)
    sine = np.sin(angles).astype(ml_dtypes.bfloat16)
    return np.stack(
        [np.stack([cosine, -sine], axis=1), np.stack([sine, cosine], axis=1)], axis=0
    )


def outer_table():
    table = dft_table(RADIX_A).transpose(2, 3, 1, 0)
    table = table.reshape(2, RADIX_A // 4, 4, RADIX_A, 2)
    grid = np.zeros((2, RADIX_A // 4, PAIR, 4, 2, 2, PAIR, RADIX_A, 2), ml_dtypes.bfloat16)
    for spectrum in range(PAIR):
        for pol in range(2):
            grid[:, :, spectrum, :, pol, pol, spectrum] = table
    return grid.reshape(2 * RADIX_A * QUAD, QUAD * ROWS)


def inner_table():
    return dft_table(RADIX_B).reshape(2 * RADIX_B, 2 * RADIX_B).T.copy()


def twiddles():
    c1 = np.zeros((RADIX_A // 4, PAIR, 4, 2), np.int64)
    c1 += np.arange(RADIX_A).reshape(RADIX_A // 4, 1, 4, 1)
    angles = (c1.reshape(-1, 1) * np.arange(RADIX_B) % LENGTH) * (2.0 * np.pi / LENGTH)
    scale = 1.0 / np.sqrt(np.float64(LENGTH))
    return np.stack([np.cos(angles) * scale, np.sin(angles) * scale]).astype(np.float32)


def spread_taps(taps_ref, taps2):
    for a in range(RADIX_A):
        for k in range(TAPS):
            row = taps_ref[k : k + 1, a * RADIX_B : (a + 1) * RADIX_B]
            taps2[k, 2 * a : 2 * a + 2, :] = jnp.broadcast_to(row, (2, RADIX_B))


def fir(first, count, base, stations, x_ref, near_ref, far_ref, taps2, filt, place):
    pieces = ROWS // 16

    def step(at, carry):
        station = at // (2 * pieces)
        pol = at // pieces % 2
        row = pl.multiple_of(at % pieces * 16, 16)
        frames = []
        for f in range(first - TAPS + 1, first + count):
            if f < -NEAR:
                where = pl.multiple_of((f + TAPS - 1) * ROWS + row, 16)
                piece = far_ref[station, pol, pl.ds(where, 16), :]
            elif f < 0:
                where = pl.multiple_of((f + NEAR) * ROWS + row, 16)
                piece = near_ref[base + station, pol, pl.ds(where, 16), :]
            else:
                where = pl.multiple_of(f * ROWS + row, 16)
                piece = x_ref[station, pol, pl.ds(where, 16), :]
            frames.append(piece.astype(F32))
        taps = [taps2[k, pl.ds(row, 16), :] for k in range(TAPS)]
        halves = []
        for half in range(2):
            rows = slice(8 * half, 8 * half + 8)
            outs = []
            for t in range(count):
                total = taps[0][rows] * frames[t][rows]
                for k in range(1, TAPS):
                    total = total + taps[k][rows] * frames[t + k][rows]
                outs.append(total)
            halves.append(outs)
        for t in range(count):
            both = jnp.concatenate([halves[0][t], halves[1][t]], axis=0).astype(BF16)
            where = pl.multiple_of(place(station, pol, t) * ROWS + row, 16)
            filt[pl.ds(where, 16), :] = both
        return carry

    lax.fori_loop(0, stations * 2 * pieces, step, 0)


def outer_stage(quads, stations, frame, outer_ref, tw_ref, mid):
    half = RADIX_A * QUAD
    cosine = tw_ref[0]
    sine = tw_ref[1]
    table = outer_ref[...]
    for first in range(0, stations * quads, 2):
        held = range(first, min(first + 2, stations * quads))
        data = []
        for n in held:
            s, q = n // quads, n % quads
            data.append([frame(s, pol, PAIR * q + t) for pol in range(2) for t in range(PAIR)])
        data = jnp.concatenate([jnp.concatenate(frames, axis=0) for frames in data], axis=1)
        got = jnp.dot(table, data, preferred_element_type=F32)
        for side, n in enumerate(held):
            s, q = n // quads, n % quads
            real = got[:half, side * 128 : side * 128 + 128]
            imag = got[half:, side * 128 : side * 128 + 128]
            real_out = (real * cosine + imag * sine).astype(BF16)
            imag_out = (imag * cosine - real * sine).astype(BF16)
            for g in range(half // 16):
                to = (s * half // 16 * quads + g * quads + q) * 16
                mid[to : to + 16, :RADIX_B] = real_out[16 * g : 16 * g + 16]
                mid[to : to + 16, RADIX_B:] = imag_out[16 * g : 16 * g + 16]


def inner_stage(quads, station, data_ref, start, inner_ref, turn):
    block = 8 * quads
    for first in range(0, quads, 2):
        wide = min(2, quads - first)
        at = start + first * 128
        got = lax.dot_general(
            inner_ref[...],
            data_ref[at : at + wide * 128, :],
            (((1,), (1,)), ((), ())),
            preferred_element_type=F32,
        )
        for side in range(wide):
            group = first + side
            for part in range(2):
                for c in range(0, RADIX_B, 8):
                    to = c * block + group * 8 + part + 2 * station
                    turn[pl.ds(to, 8, stride=block), :] = got[
                        part * RADIX_B + c : part * RADIX_B + c + 8,
                        side * 128 : side * 128 + 128,
                    ]


def send_out(turn, packed, out_ref, sems, before=None, station=0):
    rows = turn.shape[0]
    parts = sems.shape[0]
    size = rows // parts
    own = lax.broadcasted_iota(jnp.int32, (size, 128), 0) % 8 >= 2 * station
    copies = []
    for p in range(parts):
        part = pl.ds(p * size, size)
        values = turn[part, :]
        if before is not None:
            values = jnp.where(own, values, before[part, :])
        packed[part, :] = values.astype(BF16)
        copy = pltpu.make_async_copy(packed.at[part], out_ref.at[part], sems.at[p])
        copy.start()
        copies.append(copy)
    for copy in copies:
        copy.wait()


def fetch(pairs, sems):
    copies = [pltpu.make_async_copy(a, b, sems.at[i]) for i, (a, b) in enumerate(pairs)]
    for copy in copies:
        copy.start()
    return copies


def rows_of(filt, block):
    return filt[block * ROWS : (block + 1) * ROWS, :]


def first_body(first, count, stations, x_ref, taps2, filt):
    fir(first, count, 0, stations, x_ref, None, None, taps2, filt, lambda s, pol, t: (s * 2 + pol) * count + t)


def early_body(
    first, count, quads, stations, x_ref, near_ref, taps2, before, outer_hbm, tw_hbm, inner_hbm, out_ref,
    outer_ref, tw_ref, inner_ref, filt, mid, turn, packed, sems, in_sems,
):
    copies = fetch([(outer_hbm, outer_ref), (tw_hbm, tw_ref), (inner_hbm, inner_ref)], in_sems)
    fir(first, NEAR, 0, stations, x_ref, near_ref, None, taps2, filt, lambda s, pol, t: (s * 2 + pol) * NEAR + t)
    for copy in copies:
        copy.wait()

    def frame(s, pol, t):
        if t < NEAR:
            return rows_of(filt, (s * 2 + pol) * NEAR + t)
        return rows_of(before, (s * 2 + pol) * (count - NEAR) + t - NEAR)

    outer_stage(quads, stations, frame, outer_ref, tw_ref, mid)
    for s in range(stations):
        inner_stage(quads, s, mid, s * 128 * quads, inner_ref, turn)
    send_out(turn, packed, out_ref, sems)


def late_body(
    last, count, quads, base, stations, x_ref, near_ref, far_ref, taps2, outer_hbm, tw_hbm, inner_hbm, *refs
):
    if last:
        before, out_ref, outer_ref, tw_ref, inner_ref, filt, mid, in_sems, turn, packed, sems = refs
    else:
        turn, outer_ref, tw_ref, inner_ref, filt, mid, in_sems, held, held_sem = refs
        copy = pltpu.make_async_copy(x_ref.at[pl.ds(base, stations), :, pl.ds(0, held.shape[2])], held, held_sem)
        copy.start()
        copy.wait()
        x_ref = held

    def place(s, pol, t):
        return (s * 2 + pol) * count + t

    copies = fetch([(outer_hbm, outer_ref), (tw_hbm, tw_ref), (inner_hbm, inner_ref)], in_sems)
    fir(0, count, base, stations, x_ref, near_ref, far_ref, taps2, filt, place)
    for copy in copies:
        copy.wait()
    outer_stage(quads, stations, lambda *at: rows_of(filt, place(*at)), outer_ref, tw_ref, mid)
    for s in range(stations):
        inner_stage(quads, base + s, mid, s * 128 * quads, inner_ref, turn)
    if last:
        send_out(turn, packed, out_ref, sems, before, base)


def filter_first(x, taps2, first, count):
    stations = x.shape[0]
    return pl.pallas_call(
        functools.partial(first_body, first, count, stations),
        out_shape=jax.ShapeDtypeStruct((stations * 2 * count * ROWS, RADIX_B), BF16),
        in_specs=[IN_VMEM, IN_VMEM],
        out_specs=IN_VMEM,
        compiler_params=params(),
        cost_estimate=HEAVY,
    )(x, taps2)


def channelise_early(x, near, taps2, before, tables, first, count):
    stations = x.shape[0]
    quads = 2 * count // QUAD
    rows = RADIX_B * 8 * quads
    return pl.pallas_call(
        functools.partial(early_body, first, count, quads, stations),
        out_shape=pltpu.HBM((rows, 128), BF16),
        in_specs=[IN_VMEM] * 4 + [IN_HBM] * 3,
        out_specs=IN_HBM,
        scratch_shapes=[pltpu.VMEM(table.shape, table.dtype) for table in tables]
        + [
            pltpu.VMEM((stations * 2 * NEAR * ROWS, RADIX_B), BF16),
            pltpu.VMEM((stations * 128 * quads, 2 * RADIX_B), BF16),
            pltpu.VMEM((rows, 128), F32),
            pltpu.VMEM((rows, 128), BF16),
            pltpu.SemaphoreType.DMA((4,)),
            pltpu.SemaphoreType.DMA((3,)),
        ],
        compiler_params=params(),
        cost_estimate=SOME,
    )(x, near, taps2, before, *map(in_hbm, tables))


def channelise_late(x, near, far, taps2, tables, base, count, before=None):
    stations = far.shape[0]
    quads = 2 * count // QUAD
    rows = RADIX_B * 8 * quads
    last = before is not None
    scratch = [pltpu.VMEM(table.shape, table.dtype) for table in tables] + [
        pltpu.VMEM((stations * 2 * count * ROWS, RADIX_B), BF16),
        pltpu.VMEM((stations * 128 * quads, 2 * RADIX_B), BF16),
        pltpu.SemaphoreType.DMA((3,)),
    ]
    if last:
        scratch += [
            pltpu.VMEM((rows, 128), F32),
            pltpu.VMEM((rows, 128), BF16),
            pltpu.SemaphoreType.DMA((8,)),
        ]
    else:
        scratch += [pltpu.VMEM((stations, 2, count * ROWS, RADIX_B), BF16), pltpu.SemaphoreType.DMA]
    return pl.pallas_call(
        functools.partial(late_body, last, count, quads, base, stations),
        out_shape=pltpu.HBM((rows, 128), BF16) if last else jax.ShapeDtypeStruct((rows, 128), F32),
        in_specs=[IN_VMEM if last else IN_HBM] + [IN_VMEM] * 3 + [IN_HBM] * 3 + [IN_VMEM] * last,
        out_specs=IN_HBM if last else IN_VMEM,
        scratch_shapes=scratch,
        compiler_params=params(),
        cost_estimate=HEAVY if last else LIGHT,
    )(x if last else in_hbm(x), near, far, taps2, *map(in_hbm, tables), *([before] if last else []))


def history_body(starts, x_ref, *refs):
    count = len(starts)
    taps_ref = taps2 = None
    if len(refs) > 2 * count + 2:
        taps_hbm, refs = refs[0], refs[1:]
        taps2 = refs[count]
        refs = refs[:count] + refs[count + 1 :]
        taps_ref, taps_sem, refs = refs[-2], refs[-1], refs[:-2]
        taps_copy = pltpu.make_async_copy(taps_hbm, taps_ref, taps_sem)
        taps_copy.start()
    outs, helds, sems, out_sems = refs[:count], refs[count : 2 * count], refs[-2], refs[-1]
    pieces = []
    for (station, start), out, held in zip(starts, outs, helds):
        for s in range(out.shape[0]):
            at = len(pieces)
            source = x_ref.at[station + s, :, pl.ds(start, out.shape[2])]
            into = pltpu.make_async_copy(source, held.at[s], sems.at[at])
            onward = pltpu.make_async_copy(held.at[s], out.at[s], out_sems.at[at])
            into.start()
            pieces.append((into, onward))
    for into, onward in pieces:
        into.wait()
        onward.start()
    if taps_ref is not None:
        taps_copy.wait()
        spread_taps(taps_ref, taps2)
    for _, onward in pieces:
        onward.wait()


def history(x, parts, taps=None):
    shapes = [(n, 2, frames * ROWS, RADIX_B) for _, n, _, frames in parts]
    starts = [(station, frame * ROWS) for station, _, frame, _ in parts]
    pieces = sum(n for _, n, _, _ in parts)
    operands, in_specs, fetch = [in_hbm(x)], [IN_HBM], []
    out_shape = [pltpu.HBM(shape, BF16) for shape in shapes]
    out_specs = [IN_HBM] * len(parts)
    if taps is not None:
        operands.append(in_hbm(taps))
        in_specs.append(IN_HBM)
        fetch = [pltpu.VMEM(taps.shape, F32), pltpu.SemaphoreType.DMA]
        out_shape.append(jax.ShapeDtypeStruct((TAPS, ROWS, RADIX_B), F32))
        out_specs.append(IN_VMEM)
    return pl.pallas_call(
        functools.partial(history_body, starts),
        out_shape=out_shape,
        in_specs=in_specs,
        out_specs=out_specs,
        scratch_shapes=[pltpu.VMEM(shape, BF16) for shape in shapes]
        + [pltpu.SemaphoreType.DMA((pieces,))] * 2
        + fetch,
        compiler_params=params(),
        cost_estimate=LIGHT,
    )(*operands)


def weights_body(upper_ref, codes_ref, scale_ref, near_ref, far_hbm, far_ref, sem):
    upper = upper_ref[0]
    unit = 2.0 * np.pi / LENGTH

    def step(at, carry):
        row = pl.multiple_of(at // 8 * 16, 16)
        col = pl.multiple_of(at % 8 * 128, 128)
        codes = codes_ref[pl.ds(row, 16), pl.ds(col, 128)]
        scale = scale_ref[:, pl.ds(col, 128)]
        start = ((codes * (upper * RADIX_A)) & (LENGTH - 1)).astype(F32) * unit
        by = codes.astype(F32) * unit
        odd = (lax.broadcasted_iota(jnp.int32, (16, 128), 1) & 1) == 1
        cosine = jnp.cos(start) * scale
        sine = jnp.sin(start) * scale
        here = jnp.where(odd, sine, cosine)
        across = jnp.where(odd, cosine, -sine)
        by_cos = jnp.cos(by)
        by_sin = jnp.sin(by)
        for c1 in range(RADIX_A):
            to_ref, at_c1 = (near_ref, c1) if c1 < KEPT else (far_ref, c1 - KEPT)
            to_ref[at_c1, pl.ds(row, 16), pl.ds(col, 128)] = here.astype(BF16)
            if c1 + 1 < RADIX_A:
                here, across = here * by_cos + across * by_sin, across * by_cos - here * by_sin
        return carry

    lax.fori_loop(0, 32, step, 0)
    copy = pltpu.make_async_copy(far_ref, far_hbm, sem)
    copy.start()
    copy.wait()


def beam_weights(upper, codes, flags):
    beam_count, stations = codes.shape
    codes = jnp.repeat(codes, 2, axis=1)
    scale = flags.astype(F32) / jnp.sqrt(jnp.float32(stations))
    scale = jnp.repeat(scale, 2)[None, :]
    shape = (RADIX_A - KEPT, beam_count, 2 * stations)
    return pl.pallas_call(
        weights_body,
        out_shape=[pltpu.VMEM((KEPT,) + shape[1:], BF16), pltpu.HBM(shape, BF16)],
        in_specs=[pl.BlockSpec(memory_space=pltpu.SMEM), IN_VMEM, IN_VMEM],
        out_specs=[IN_VMEM, IN_HBM],
        scratch_shapes=[pltpu.VMEM(shape, BF16), pltpu.SemaphoreType.DMA],
        compiler_params=params(),
        cost_estimate=LIGHT,
    )(upper, codes, scale)


def beams_body(quads, last, x_ref, near_ref, far_hbm, *refs):
    if last:
        early_hbm, out_ref, total, far_ref, sems, early_ref, early_sem = refs
        early_copy = pltpu.make_async_copy(early_hbm, early_ref, early_sem)
    else:
        out_hbm, total, far_ref, sems, out_sem = refs
    size = far_ref.shape[0] // sems.shape[0]
    parts = [pl.ds(i * size, size) for i in range(sems.shape[0])]
    copies = fetch([(far_hbm.at[part], far_ref.at[part]) for part in parts], sems)
    if last:
        early_copy.start()
    here = False
    beam_count = near_ref.shape[1]
    spectra = total.shape[0] // (2 * RADIX_A)
    lane = lax.broadcasted_iota(jnp.int32, (1, 128), 1)
    even = (lax.broadcasted_iota(jnp.int32, (1, 8, 128), 1) & 1) == 0
    for group in range(quads):
        base = group * 128
        low = base // (16 * quads)
        high = (base + 127) // (16 * quads)
        values = x_ref[:, group]
        wide = values.astype(F32)
        swapped = jnp.where(even, pltpu.roll(wide, 7, 1), -pltpu.roll(wide, 1, 1)).astype(BF16)
        data = jnp.concatenate([values.reshape(1024, 128), swapped.reshape(1024, 128)], axis=1)
        c1 = (base + lane) // (16 * quads) * 4 + lane % 8 // 2
        real = imag = None
        for g in range(low, high + 1):
            first = 4 * g
            if first < KEPT:
                weights = near_ref[first : first + 4]
            else:
                if not here:
                    for copy in copies:
                        copy.wait()
                    here = True
                weights = far_ref[first - KEPT : first - KEPT + 4]
            weights = weights.reshape(4 * beam_count, 1024)
            got = jnp.dot(weights, data, preferred_element_type=F32)
            for c in range(4):
                piece = got[beam_count * c : beam_count * (c + 1)]
                if real is None:
                    real, imag = piece[:, :128], piece[:, 128:]
                else:
                    mine = c1 == 4 * g + c
                    real = jnp.where(mine, piece[:, :128], real)
                    imag = jnp.where(mine, piece[:, 128:], imag)
        turned = jnp.concatenate([real, imag], axis=0).T
        for m in range(0, 128, 8):
            at = base + m
            block = at // (16 * quads)
            t = at % (16 * quads) // 16 * PAIR + at % 16 // 8
            total[pl.ds(block * 8 * spectra + t, 8, stride=spectra), :] = turned[m : m + 8]
    if last:
        early_copy.wait()
        early = early_ref.shape[0] // (2 * RADIX_A)
        for t in range(early):
            for row in range(0, 2 * RADIX_A, 8):
                total[pl.ds((row + 1) * spectra - early + t, 8, stride=spectra), :] = early_ref[
                    pl.ds(row * early + t, 8, stride=early), :
                ]
        out_ref[...] = total[...].astype(BF16)
    else:
        out_copy = pltpu.make_async_copy(total, out_hbm, out_sem)
        out_copy.start()
        out_copy.wait()


def beams(received, weights, quads, early):
    count = quads * QUAD // 2
    received = received.reshape(RADIX_B, quads, 8, 128)
    kept, others = weights
    operands = [received, pltpu.with_memory_space_constraint(kept, pltpu.VMEM), in_hbm(others)]
    in_specs = [IN_VMEM, IN_VMEM, IN_HBM]
    last = early is not None
    shape = (2 * RADIX_A * count + (early.shape[0] if last else 0), 128)
    scratch = [pltpu.VMEM(shape, F32), pltpu.VMEM(others.shape, BF16), pltpu.SemaphoreType.DMA((8,))]
    if last:
        operands.append(in_hbm(early))
        in_specs.append(IN_HBM)
        scratch += [pltpu.VMEM(early.shape, F32)]
    scratch += [pltpu.SemaphoreType.DMA]
    return pl.pallas_call(
        functools.partial(beams_body, quads, last),
        out_shape=jax.ShapeDtypeStruct(shape, BF16) if last else pltpu.HBM(shape, F32),
        in_specs=in_specs,
        out_specs=IN_VMEM if last else IN_HBM,
        scratch_shapes=scratch,
        compiler_params=params(),
        cost_estimate=LIGHT,
    )(*operands)


def turn(spectra):
    spectra = spectra.reshape(RADIX_B, -1, 128)
    return lax.all_to_all(spectra, "stn", split_axis=0, concat_axis=0, tiled=True)


def shards(samples, taps, codes, flags):
    stations = samples.shape[0]
    frames = samples.shape[3] // LENGTH
    size = lax.axis_size("tm")
    x = samples.reshape(stations, 2, 2, frames * RADIX_A, RADIX_B)
    x = x.transpose(0, 1, 3, 2, 4).reshape(stations, 2, frames * ROWS, RADIX_B)
    pairs = [(i, i + 1) for i in range(size - 1)]
    lead = stations - 1
    rest = frames - TAPS + 1, TAPS - 1 - NEAR
    parts = [(0, stations, frames - NEAR, NEAR), (0, lead, *rest), (lead, 1, *rest)]
    near, far, far_last, taps2 = history(x, parts, taps)
    near = lax.ppermute(near, "tm", pairs)
    far = lax.ppermute(far, "tm", pairs)

    tables = (jnp.asarray(outer_table()), jnp.asarray(twiddles()), jnp.asarray(inner_table()))
    late = frames - EARLY
    filtered = filter_first(x, taps2, late + NEAR, EARLY - NEAR)
    filtered, far_last = lax.optimization_barrier((filtered, far_last))
    early_sent = channelise_early(x, near, taps2, filtered, tables, late, EARLY)
    early_got = turn(early_sent)
    far_last = lax.ppermute(far_last, "tm", pairs)
    upper = lax.axis_index("stn").astype(jnp.int32).reshape(1)
    weights = beam_weights(upper, codes, flags)
    ahead = channelise_late(x, near, far, taps2, tables, 0, late)
    main_sent = channelise_late(x[lead:, :, : late * ROWS], near, far_last, taps2, tables, lead, late, ahead)
    main_got = turn(main_sent)
    early = beams(early_got, weights, EARLY // PAIR, None)
    result = beams(main_got, weights, late // PAIR, early)
    return result.reshape(RADIX_A, 2, frames, 128)


def solution(mesh):
    in_specs = (P("stn", None, None, "tm"), P(), P(), P())
    out_specs = P("stn", None, "tm", None)
    return jax.shard_map(shards, mesh=mesh, in_specs=in_specs, out_specs=out_specs, check_vma=False)
```

```python
import functools

import jax
import jax.numpy as jnp
import ml_dtypes
import numpy as np
from jax import lax
from jax.experimental import pallas as pl
from jax.experimental.pallas import tpu as pltpu
from jax.sharding import PartitionSpec as P

RADIX_A = 32
RADIX_B = 128
TAPS = 12
LENGTH = RADIX_A * RADIX_B
ROWS = 2 * RADIX_A
PAIR = 2
QUAD = 2 * PAIR
KEPT = 16
NEAR = 1
EARLY = TAPS - 7 + NEAR
BF16 = jnp.bfloat16
F32 = jnp.float32
VMEM_LIMIT = 16 << 20


def params():
    return pltpu.CompilerParams(vmem_limit_bytes=VMEM_LIMIT)


def in_hbm(array):
    return pltpu.with_memory_space_constraint(array, pltpu.HBM)


IN_VMEM = pl.BlockSpec(memory_space=pltpu.VMEM)
IN_HBM = pl.BlockSpec(memory_space=pltpu.HBM)
LIGHT = pl.CostEstimate(flops=1024, bytes_accessed=1024, transcendentals=0)
SOME = pl.CostEstimate(flops=7 << 30, bytes_accessed=1024, transcendentals=0)
HEAVY = pl.CostEstimate(flops=1 << 37, bytes_accessed=1024, transcendentals=0)


def dft_table(radix):
    indices = np.arange(radix)
    angles = (indices[:, None] * indices[None, :] % radix) * (2.0 * np.pi / radix)
    cosine = np.cos(angles).astype(ml_dtypes.bfloat16)
    sine = np.sin(angles).astype(ml_dtypes.bfloat16)
    return np.stack(
        [np.stack([cosine, -sine], axis=1), np.stack([sine, cosine], axis=1)], axis=0
    )


def outer_table():
    table = dft_table(RADIX_A).transpose(2, 3, 1, 0)
    table = table.reshape(2, RADIX_A // 4, 4, RADIX_A, 2)
    grid = np.zeros((2, RADIX_A // 4, PAIR, 4, 2, 2, PAIR, RADIX_A, 2), ml_dtypes.bfloat16)
    for spectrum in range(PAIR):
        for pol in range(2):
            grid[:, :, spectrum, :, pol, pol, spectrum] = table
    return grid.reshape(2 * RADIX_A * QUAD, QUAD * ROWS)


def inner_table():
    return dft_table(RADIX_B).reshape(2 * RADIX_B, 2 * RADIX_B).T.copy()


def twiddles():
    c1 = np.zeros((RADIX_A // 4, PAIR, 4, 2), np.int64)
    c1 += np.arange(RADIX_A).reshape(RADIX_A // 4, 1, 4, 1)
    angles = (c1.reshape(-1, 1) * np.arange(RADIX_B) % LENGTH) * (2.0 * np.pi / LENGTH)
    scale = 1.0 / np.sqrt(np.float64(LENGTH))
    return np.stack([np.cos(angles) * scale, np.sin(angles) * scale]).astype(np.float32)


def spread_taps(taps_ref, taps2):
    for a in range(RADIX_A):
        for k in range(TAPS):
            row = taps_ref[k : k + 1, a * RADIX_B : (a + 1) * RADIX_B]
            taps2[k, 2 * a : 2 * a + 2, :] = jnp.broadcast_to(row, (2, RADIX_B))


def fir(first, count, base, stations, x_ref, near_ref, far_ref, taps2, filt, place):
    pieces = ROWS // 16

    def step(at, carry):
        station = at // (2 * pieces)
        pol = at // pieces % 2
        row = pl.multiple_of(at % pieces * 16, 16)
        frames = []
        for f in range(first - TAPS + 1, first + count):
            if f < -NEAR:
                where = pl.multiple_of((f + TAPS - 1) * ROWS + row, 16)
                piece = far_ref[station, pol, pl.ds(where, 16), :]
            elif f < 0:
                where = pl.multiple_of((f + NEAR) * ROWS + row, 16)
                piece = near_ref[base + station, pol, pl.ds(where, 16), :]
            else:
                where = pl.multiple_of(f * ROWS + row, 16)
                piece = x_ref[station, pol, pl.ds(where, 16), :]
            frames.append(piece.astype(F32))
        taps = [taps2[k, pl.ds(row, 16), :] for k in range(TAPS)]
        halves = []
        for half in range(2):
            rows = slice(8 * half, 8 * half + 8)
            outs = []
            for t in range(count):
                total = taps[0][rows] * frames[t][rows]
                for k in range(1, TAPS):
                    total = total + taps[k][rows] * frames[t + k][rows]
                outs.append(total)
            halves.append(outs)
        for t in range(count):
            both = jnp.concatenate([halves[0][t], halves[1][t]], axis=0).astype(BF16)
            where = pl.multiple_of(place(station, pol, t) * ROWS + row, 16)
            filt[pl.ds(where, 16), :] = both
        return carry

    lax.fori_loop(0, stations * 2 * pieces, step, 0)


def outer_stage(quads, stations, frame, outer_ref, tw_ref, mid):
    half = RADIX_A * QUAD
    cosine = tw_ref[0]
    sine = tw_ref[1]
    table = outer_ref[...]
    for first in range(0, stations * quads, 2):
        held = range(first, min(first + 2, stations * quads))
        data = []
        for n in held:
            s, q = n // quads, n % quads
            data.append([frame(s, pol, PAIR * q + t) for pol in range(2) for t in range(PAIR)])
        data = jnp.concatenate([jnp.concatenate(frames, axis=0) for frames in data], axis=1)
        got = jnp.dot(table, data, preferred_element_type=F32)
        for side, n in enumerate(held):
            s, q = n // quads, n % quads
            real = got[:half, side * 128 : side * 128 + 128]
            imag = got[half:, side * 128 : side * 128 + 128]
            real_out = (real * cosine + imag * sine).astype(BF16)
            imag_out = (imag * cosine - real * sine).astype(BF16)
            for g in range(half // 16):
                to = (s * half // 16 * quads + g * quads + q) * 16
                mid[to : to + 16, :RADIX_B] = real_out[16 * g : 16 * g + 16]
                mid[to : to + 16, RADIX_B:] = imag_out[16 * g : 16 * g + 16]


def inner_stage(quads, station, data_ref, start, inner_ref, turn):
    block = 8 * quads
    for first in range(0, quads, 2):
        wide = min(2, quads - first)
        at = start + first * 128
        got = lax.dot_general(
            inner_ref[...],
            data_ref[at : at + wide * 128, :],
            (((1,), (1,)), ((), ())),
            preferred_element_type=F32,
        )
        for side in range(wide):
            group = first + side
            for part in range(2):
                for c in range(0, RADIX_B, 8):
                    to = c * block + group * 8 + part + 2 * station
                    turn[pl.ds(to, 8, stride=block), :] = got[
                        part * RADIX_B + c : part * RADIX_B + c + 8,
                        side * 128 : side * 128 + 128,
                    ]


def send_out(turn, packed, out_ref, sems, before=None, station=0):
    rows = turn.shape[0]
    parts = sems.shape[0]
    size = rows // parts
    own = lax.broadcasted_iota(jnp.int32, (size, 128), 0) % 8 >= 2 * station
    copies = []
    for p in range(parts):
        part = pl.ds(p * size, size)
        values = turn[part, :]
        if before is not None:
            values = jnp.where(own, values, before[part, :])
        packed[part, :] = values.astype(BF16)
        copy = pltpu.make_async_copy(packed.at[part], out_ref.at[part], sems.at[p])
        copy.start()
        copies.append(copy)
    for copy in copies:
        copy.wait()


def fetch(pairs, sems):
    copies = [pltpu.make_async_copy(a, b, sems.at[i]) for i, (a, b) in enumerate(pairs)]
    for copy in copies:
        copy.start()
    return copies


def rows_of(filt, block):
    return filt[block * ROWS : (block + 1) * ROWS, :]


def first_body(first, count, stations, x_ref, taps2, filt):
    fir(first, count, 0, stations, x_ref, None, None, taps2, filt, lambda s, pol, t: (s * 2 + pol) * count + t)


def early_body(
    first, count, quads, stations, x_ref, near_ref, taps2, before, outer_hbm, tw_hbm, inner_hbm, out_ref,
    outer_ref, tw_ref, inner_ref, filt, mid, turn, packed, sems, in_sems,
):
    copies = fetch([(outer_hbm, outer_ref), (tw_hbm, tw_ref), (inner_hbm, inner_ref)], in_sems)
    fir(first, NEAR, 0, stations, x_ref, near_ref, None, taps2, filt, lambda s, pol, t: (s * 2 + pol) * NEAR + t)
    copies[0].wait()
    copies[1].wait()

    def frame(s, pol, t):
        if t < NEAR:
            return rows_of(filt, (s * 2 + pol) * NEAR + t)
        return rows_of(before, (s * 2 + pol) * (count - NEAR) + t - NEAR)

    outer_stage(quads, stations, frame, outer_ref, tw_ref, mid)
    copies[2].wait()
    for s in range(stations):
        inner_stage(quads, s, mid, s * 128 * quads, inner_ref, turn)
    send_out(turn, packed, out_ref, sems)


def late_body(
    last, count, quads, base, stations, x_ref, near_ref, far_ref, taps2, outer, tw, inner, *refs
):
    if last:
        before, out_ref, filt, mid, turn, packed, sems = refs
        copies = []
    else:
        turn, *tables, filt, mid, in_sems, held, held_sem = refs
        copies = fetch(list(zip((outer, tw, inner), tables)), in_sems)
        outer, tw, inner = tables
        copy = pltpu.make_async_copy(x_ref.at[pl.ds(base, stations), :, pl.ds(0, held.shape[2])], held, held_sem)
        copy.start()
        copy.wait()
        x_ref = held

    def place(s, pol, t):
        return (s * 2 + pol) * count + t

    fir(0, count, base, stations, x_ref, near_ref, far_ref, taps2, filt, place)
    for copy in copies:
        copy.wait()
    outer_stage(quads, stations, lambda *at: rows_of(filt, place(*at)), outer, tw, mid)
    for s in range(stations):
        inner_stage(quads, base + s, mid, s * 128 * quads, inner, turn)
    if last:
        send_out(turn, packed, out_ref, sems, before, base)


def filter_first(x, taps2, first, count):
    stations = x.shape[0]
    return pl.pallas_call(
        functools.partial(first_body, first, count, stations),
        out_shape=jax.ShapeDtypeStruct((stations * 2 * count * ROWS, RADIX_B), BF16),
        in_specs=[IN_VMEM, IN_VMEM],
        out_specs=IN_VMEM,
        compiler_params=params(),
        cost_estimate=HEAVY,
    )(x, taps2)


def channelise_early(x, near, taps2, before, tables, first, count):
    stations = x.shape[0]
    quads = 2 * count // QUAD
    rows = RADIX_B * 8 * quads
    return pl.pallas_call(
        functools.partial(early_body, first, count, quads, stations),
        out_shape=pltpu.HBM((rows, 128), BF16),
        in_specs=[IN_VMEM] * 4 + [IN_HBM] * 3,
        out_specs=IN_HBM,
        scratch_shapes=[pltpu.VMEM(table.shape, table.dtype) for table in tables]
        + [
            pltpu.VMEM((stations * 2 * NEAR * ROWS, RADIX_B), BF16),
            pltpu.VMEM((stations * 128 * quads, 2 * RADIX_B), BF16),
            pltpu.VMEM((rows, 128), F32),
            pltpu.VMEM((rows, 128), BF16),
            pltpu.SemaphoreType.DMA((4,)),
            pltpu.SemaphoreType.DMA((3,)),
        ],
        compiler_params=params(),
        cost_estimate=SOME,
    )(x, near, taps2, before, *map(in_hbm, tables))


def channelise_late(x, near, far, taps2, tables, base, count, before=None):
    stations = far.shape[0]
    quads = 2 * count // QUAD
    rows = RADIX_B * 8 * quads
    last = before is not None
    scratch = [
        pltpu.VMEM((stations * 2 * count * ROWS, RADIX_B), BF16),
        pltpu.VMEM((stations * 128 * quads, 2 * RADIX_B), BF16),
    ]
    if last:
        scratch += [
            pltpu.VMEM((rows, 128), F32),
            pltpu.VMEM((rows, 128), BF16),
            pltpu.SemaphoreType.DMA((8,)),
        ]
        out_shape = pltpu.HBM((rows, 128), BF16)
    else:
        scratch += [
            pltpu.SemaphoreType.DMA((3,)),
            pltpu.VMEM((stations, 2, count * ROWS, RADIX_B), BF16),
            pltpu.SemaphoreType.DMA,
        ]
        out_shape = [jax.ShapeDtypeStruct((rows, 128), F32)]
        out_shape += [jax.ShapeDtypeStruct(table.shape, table.dtype) for table in tables]
        x, tables = in_hbm(x), tuple(map(in_hbm, tables))
    home = IN_VMEM if last else IN_HBM
    return pl.pallas_call(
        functools.partial(late_body, last, count, quads, base, stations),
        out_shape=out_shape,
        in_specs=[home] + [IN_VMEM] * 3 + [home] * 3 + [IN_VMEM] * last,
        out_specs=IN_HBM if last else [IN_VMEM] * 4,
        scratch_shapes=scratch,
        compiler_params=params(),
        cost_estimate=HEAVY if last else LIGHT,
    )(x, near, far, taps2, *tables, *([before] if last else []))


def history_body(starts, x_ref, *refs):
    count = len(starts)
    taps_ref = taps2 = None
    if len(refs) > 2 * count + 2:
        taps_hbm, refs = refs[0], refs[1:]
        taps2 = refs[count]
        refs = refs[:count] + refs[count + 1 :]
        taps_ref, taps_sem, refs = refs[-2], refs[-1], refs[:-2]
        taps_copy = pltpu.make_async_copy(taps_hbm, taps_ref, taps_sem)
        taps_copy.start()
    outs, helds, sems, out_sems = refs[:count], refs[count : 2 * count], refs[-2], refs[-1]
    pieces = []
    for (station, start), out, held in zip(starts, outs, helds):
        for s in range(out.shape[0]):
            at = len(pieces)
            source = x_ref.at[station + s, :, pl.ds(start, out.shape[2])]
            into = pltpu.make_async_copy(source, held.at[s], sems.at[at])
            onward = pltpu.make_async_copy(held.at[s], out.at[s], out_sems.at[at])
            into.start()
            pieces.append((into, onward))
    for into, onward in pieces:
        into.wait()
        onward.start()
    if taps_ref is not None:
        taps_copy.wait()
        spread_taps(taps_ref, taps2)
    for _, onward in pieces:
        onward.wait()


def history(x, parts, taps=None):
    shapes = [(n, 2, frames * ROWS, RADIX_B) for _, n, _, frames in parts]
    starts = [(station, frame * ROWS) for station, _, frame, _ in parts]
    pieces = sum(n for _, n, _, _ in parts)
    operands, in_specs, fetch = [in_hbm(x)], [IN_HBM], []
    out_shape = [pltpu.HBM(shape, BF16) for shape in shapes]
    out_specs = [IN_HBM] * len(parts)
    if taps is not None:
        operands.append(in_hbm(taps))
        in_specs.append(IN_HBM)
        fetch = [pltpu.VMEM(taps.shape, F32), pltpu.SemaphoreType.DMA]
        out_shape.append(jax.ShapeDtypeStruct((TAPS, ROWS, RADIX_B), F32))
        out_specs.append(IN_VMEM)
    return pl.pallas_call(
        functools.partial(history_body, starts),
        out_shape=out_shape,
        in_specs=in_specs,
        out_specs=out_specs,
        scratch_shapes=[pltpu.VMEM(shape, BF16) for shape in shapes]
        + [pltpu.SemaphoreType.DMA((pieces,))] * 2
        + fetch,
        compiler_params=params(),
        cost_estimate=LIGHT,
    )(*operands)


def weights_body(upper_ref, codes_ref, scale_ref, near_ref, far_hbm, far_ref, sem):
    upper = upper_ref[0]
    unit = 2.0 * np.pi / LENGTH

    def step(at, carry):
        row = pl.multiple_of(at // 8 * 16, 16)
        col = pl.multiple_of(at % 8 * 128, 128)
        codes = codes_ref[pl.ds(row, 16), pl.ds(col, 128)]
        scale = scale_ref[:, pl.ds(col, 128)]
        start = ((codes * (upper * RADIX_A)) & (LENGTH - 1)).astype(F32) * unit
        by = codes.astype(F32) * unit
        odd = (lax.broadcasted_iota(jnp.int32, (16, 128), 1) & 1) == 1
        cosine = jnp.cos(start) * scale
        sine = jnp.sin(start) * scale
        here = jnp.where(odd, sine, cosine)
        across = jnp.where(odd, cosine, -sine)
        by_cos = jnp.cos(by)
        by_sin = jnp.sin(by)
        for c1 in range(RADIX_A):
            to_ref, at_c1 = (near_ref, c1) if c1 < KEPT else (far_ref, c1 - KEPT)
            to_ref[at_c1, pl.ds(row, 16), pl.ds(col, 128)] = here.astype(BF16)
            if c1 + 1 < RADIX_A:
                here, across = here * by_cos + across * by_sin, across * by_cos - here * by_sin
        return carry

    lax.fori_loop(0, 32, step, 0)
    copy = pltpu.make_async_copy(far_ref, far_hbm, sem)
    copy.start()
    copy.wait()


def beam_weights(upper, codes, flags):
    beam_count, stations = codes.shape
    codes = jnp.repeat(codes, 2, axis=1)
    scale = flags.astype(F32) / jnp.sqrt(jnp.float32(stations))
    scale = jnp.repeat(scale, 2)[None, :]
    shape = (RADIX_A - KEPT, beam_count, 2 * stations)
    return pl.pallas_call(
        weights_body,
        out_shape=[pltpu.VMEM((KEPT,) + shape[1:], BF16), pltpu.HBM(shape, BF16)],
        in_specs=[pl.BlockSpec(memory_space=pltpu.SMEM), IN_VMEM, IN_VMEM],
        out_specs=[IN_VMEM, IN_HBM],
        scratch_shapes=[pltpu.VMEM(shape, BF16), pltpu.SemaphoreType.DMA],
        compiler_params=params(),
        cost_estimate=LIGHT,
    )(upper, codes, scale)


def beams_body(quads, last, x_ref, near_ref, far_hbm, *refs):
    if last:
        early_hbm, out_ref, total, far_ref, sems, early_ref, early_sem = refs
        early_copy = pltpu.make_async_copy(early_hbm, early_ref, early_sem)
    else:
        out_hbm, total, far_ref, sems, out_sem = refs
    size = far_ref.shape[0] // sems.shape[0]
    parts = [pl.ds(i * size, size) for i in range(sems.shape[0])]
    copies = fetch([(far_hbm.at[part], far_ref.at[part]) for part in parts], sems)
    if last:
        early_copy.start()
    here = False
    beam_count = near_ref.shape[1]
    spectra = total.shape[0] // (2 * RADIX_A)
    lane = lax.broadcasted_iota(jnp.int32, (1, 128), 1)
    even = (lax.broadcasted_iota(jnp.int32, (1, 8, 128), 1) & 1) == 0
    for group in range(quads):
        base = group * 128
        low = base // (16 * quads)
        high = (base + 127) // (16 * quads)
        values = x_ref[:, group]
        wide = values.astype(F32)
        swapped = jnp.where(even, pltpu.roll(wide, 7, 1), -pltpu.roll(wide, 1, 1)).astype(BF16)
        data = jnp.concatenate([values.reshape(1024, 128), swapped.reshape(1024, 128)], axis=1)
        c1 = (base + lane) // (16 * quads) * 4 + lane % 8 // 2
        real = imag = None
        for g in range(low, high + 1):
            first = 4 * g
            if first < KEPT:
                weights = near_ref[first : first + 4]
            else:
                if not here:
                    for copy in copies:
                        copy.wait()
                    here = True
                weights = far_ref[first - KEPT : first - KEPT + 4]
            weights = weights.reshape(4 * beam_count, 1024)
            got = jnp.dot(weights, data, preferred_element_type=F32)
            for c in range(4):
                piece = got[beam_count * c : beam_count * (c + 1)]
                if real is None:
                    real, imag = piece[:, :128], piece[:, 128:]
                else:
                    mine = c1 == 4 * g + c
                    real = jnp.where(mine, piece[:, :128], real)
                    imag = jnp.where(mine, piece[:, 128:], imag)
        turned = jnp.concatenate([real, imag], axis=0).T
        for m in range(0, 128, 8):
            at = base + m
            block = at // (16 * quads)
            t = at % (16 * quads) // 16 * PAIR + at % 16 // 8
            total[pl.ds(block * 8 * spectra + t, 8, stride=spectra), :] = turned[m : m + 8]
    if last:
        early_copy.wait()
        early = early_ref.shape[0] // (2 * RADIX_A)
        for t in range(early):
            for row in range(0, 2 * RADIX_A, 8):
                total[pl.ds((row + 1) * spectra - early + t, 8, stride=spectra), :] = early_ref[
                    pl.ds(row * early + t, 8, stride=early), :
                ]
        out_ref[...] = total[...].astype(BF16)
    else:
        out_copy = pltpu.make_async_copy(total, out_hbm, out_sem)
        out_copy.start()
        out_copy.wait()


def beams(received, weights, quads, early):
    count = quads * QUAD // 2
    received = received.reshape(RADIX_B, quads, 8, 128)
    kept, others = weights
    operands = [received, pltpu.with_memory_space_constraint(kept, pltpu.VMEM), in_hbm(others)]
    in_specs = [IN_VMEM, IN_VMEM, IN_HBM]
    last = early is not None
    shape = (2 * RADIX_A * count + (early.shape[0] if last else 0), 128)
    scratch = [pltpu.VMEM(shape, F32), pltpu.VMEM(others.shape, BF16), pltpu.SemaphoreType.DMA((8,))]
    if last:
        operands.append(in_hbm(early))
        in_specs.append(IN_HBM)
        scratch += [pltpu.VMEM(early.shape, F32)]
    scratch += [pltpu.SemaphoreType.DMA]
    return pl.pallas_call(
        functools.partial(beams_body, quads, last),
        out_shape=jax.ShapeDtypeStruct(shape, BF16) if last else pltpu.HBM(shape, F32),
        in_specs=in_specs,
        out_specs=IN_VMEM if last else IN_HBM,
        scratch_shapes=scratch,
        compiler_params=params(),
        cost_estimate=LIGHT,
    )(*operands)


def turn(spectra):
    spectra = spectra.reshape(RADIX_B, -1, 128)
    return lax.all_to_all(spectra, "stn", split_axis=0, concat_axis=0, tiled=True)


def shards(samples, taps, codes, flags):
    stations = samples.shape[0]
    frames = samples.shape[3] // LENGTH
    size = lax.axis_size("tm")
    x = samples.reshape(stations, 2, 2, frames * RADIX_A, RADIX_B)
    x = x.transpose(0, 1, 3, 2, 4).reshape(stations, 2, frames * ROWS, RADIX_B)
    pairs = [(i, i + 1) for i in range(size - 1)]
    lead = stations - 1
    rest = frames - TAPS + 1, TAPS - 1 - NEAR
    parts = [(0, stations, frames - NEAR, NEAR), (0, lead, *rest), (lead, 1, *rest)]
    near, far, far_last, taps2 = history(x, parts, taps)
    near = lax.ppermute(near, "tm", pairs)
    far = lax.ppermute(far, "tm", pairs)

    tables = (jnp.asarray(outer_table()), jnp.asarray(twiddles()), jnp.asarray(inner_table()))
    late = frames - EARLY
    filtered = filter_first(x, taps2, late + NEAR, EARLY - NEAR)
    filtered, far_last = lax.optimization_barrier((filtered, far_last))
    early_sent = channelise_early(x, near, taps2, filtered, tables, late, EARLY)
    early_got = turn(early_sent)
    far_last = lax.ppermute(far_last, "tm", pairs)
    upper = lax.axis_index("stn").astype(jnp.int32).reshape(1)
    weights = beam_weights(upper, codes, flags)
    ahead, *tables = channelise_late(x, near, far, taps2, tables, 0, late)
    main_sent = channelise_late(x[lead:, :, : late * ROWS], near, far_last, taps2, tables, lead, late, ahead)
    main_got = turn(main_sent)
    early = beams(early_got, weights, EARLY // PAIR, None)
    result = beams(main_got, weights, late // PAIR, early)
    return result.reshape(RADIX_A, 2, frames, 128)


def solution(mesh):
    in_specs = (P("stn", None, None, "tm"), P(), P(), P())
    out_specs = P("stn", None, "tm", None)
    return jax.shard_map(shards, mesh=mesh, in_specs=in_specs, out_specs=out_specs, check_vma=False)
```
